512 devices in a mesh: dp: 8 (over x, core), expert: 64 (over z, y).
Axes of the slice: x: 4, y: 4, z: 16, core: 2. Of those that a mesh axis runs over, the one named last changes fastest.
Arguments:
- tokens: bfloat16 [8192, 4096], P(('dp', 'expert')), may hold values from -6 to 6
- route_ids: int32 [8192, 8], P(('dp', 'expert')), may hold values from 0 to 127, all different within a row; in each aligned block of 16 rows (0 to 15, 16 to 31, ...) at most 2 rows name the same one
- gate_weights: float32 [8192, 8], P(('dp', 'expert')), may hold values from 0.05 to 0.3
- tenant_ids: int32 [8192], P(('dp', 'expert')), may hold values from 0 to 3
- up_weight: bfloat16 [128, 4096, 1024], P('expert', 'dp'), may hold values from -0.09375 to 0.09375
- down_weight: bfloat16 [128, 1024, 4096], P('expert', None, 'dp'), may hold values from -0.1875 to 0.1875
- adapter_in: bfloat16 [128, 4096, 64], P('expert', 'dp'), may hold values from -0.09375 to 0.09375
- adapter_out: bfloat16 [128, 64, 1024], P('expert'), may hold values from -1.5 to 1.5
Outputs:
- mixed: bfloat16 [8192, 4096], P(('dp', 'expert'))
The draws below stay inside these ranges and needn't reach their ends.
Inputs may be any that keep to these rules, and one draw needn't show every extreme that they name: `route_ids`: the 8 experts of one token differ; among the 16 tokens of one device no expert is named more than 2 times, and some expert is named 2 times.
All inputs are finite; a program needn't handle non-finite values.
Results may differ from the reference program's by a relative error of at most 0.025.
Values may be sent and summed in bfloat16 or wider, within the bound.
No kernel may reach another device: no remote copies, remote signals or barrier semaphores. Data moves between devices by JAX's collectives and lax.ppermute only.
A program may use at most 64 MiB of HBM per device.

```python
import math
import jax
import jax.numpy as jnp
import numpy as np
from jax import lax

D = 4096
F = 1024
EXPERTS = 128
TOP = 8
TEN = 4
RANK = 16
TOK_DEV = 16
TOKENS = 8192
CAPE = 2
N_DP = 8


def plant(drawn, own_key, low, top_value):
    longest = drawn.shape.index(max(drawn.shape))
    spots = []
    for shift in (0, 1):
        where = [jax.random.randint(jax.random.fold_in(own_key, axis), (), 0, length) for axis, length in enumerate(drawn.shape)]
        where[longest] = (where[longest] + shift) % drawn.shape[longest]
        spots.append(tuple(where))
    return drawn.at[spots[0]].set(low).at[spots[1]].set(top_value)


def levels(rng, extent, split, smallest, high):
    gain = 1.0
    for axis_at, shards_of in split:
        heights = jax.random.uniform(jax.random.fold_in(jax.random.fold_in(rng, 6), axis_at), (shards_of,), jnp.float32, smallest / len(split), high / len(split))
        gain = gain * jnp.repeat(jnp.exp(heights), extent[axis_at] // shards_of).reshape((-1,) + (1,) * (len(extent) - 1 - axis_at))
    return gain


def deal_out(stream_key, own, number, rows, count, top, reach, lean):
    order = jax.random.permutation(stream_key, count)
    heavy_load, ordinary = portions_of(count, rows * top, reach, lean, True), portions_of(count, rows * top, reach, lean, False)
    places = jnp.arange(count)

    def named(sizes, rotation):
        used = int((sizes > 0).sum())
        fixed = max(1, used // 4)
        shifted = fixed + (places - fixed + rotation * (used - fixed)) % max(1, count - fixed)
        return jnp.zeros((count,), jnp.int32).at[order[jnp.where(places < fixed, places, shifted)]].set(jnp.asarray(sizes, jnp.int32))

    sizes = jnp.where(number % 4 == 0, named(heavy_load, number // 4), named(ordinary, number - number // 4 - 1))
    mixed = jax.random.permutation(jax.random.fold_in(own, 3), count)
    giver, receiver = mixed[0:count // 2 * 2:2], mixed[1:count // 2 * 2:2]
    slack = jnp.minimum(sizes[giver] - 1, reach - sizes[receiver]) // 2
    slack = jnp.where((giver == order[0]) | (receiver == order[0]) | (sizes[receiver] == 0), 0, jnp.maximum(slack, 0))
    shifted = jax.random.randint(jax.random.fold_in(own, 4), (count // 2,), 0, 1 << 20) % (slack + 1)
    sizes = sizes.at[giver].add(-shifted).at[receiver].add(shifted)
    members = jnp.searchsorted(jnp.cumsum(sizes), jnp.arange(rows * top), side="right").astype(jnp.int32)
    grid = members.reshape(top, rows).T
    grid = grid[jax.random.permutation(jax.random.fold_in(own, 1), rows)]
    rotation = jax.random.randint(jax.random.fold_in(own, 2), (rows, 1), 0, top)
    return jnp.take_along_axis(grid, (jnp.arange(top)[None, :] + rotation) % top, axis=1)


def portions_of(amount, total, bound, slope, full):
    weights = [(1 << 20) // math.isqrt(rank ** slope) + 1 for rank in range(1, amount + 1)]
    largest = bound if full else min(bound, max(-(-total // amount), total * weights[0] // sum(weights)))
    least = 1 if total - largest >= amount - 1 else 0
    counts, spare = [largest] + [least] * (amount - 1), total - largest - least * (amount - 1)
    while spare > 0:
        movable = [i for i in range(1, amount) if counts[i] < largest] or [i for i in range(1, amount) if counts[i] < bound]
        mass, budget = sum([weights[i] for i in movable]), spare
        for i in movable:
            more = min(bound - counts[i], max(1, budget * weights[i] // mass), spare)
            counts[i] = counts[i] + more
            spare = spare - more
    return np.array(counts)


def normal_values(key, dims, width, reach, pieces=(), kind=jnp.bfloat16):
    result = width * jax.random.normal(key, dims, jnp.float32)
    if pieces:
        result = result * levels(key, dims, pieces, -0.22, 0.18)
    return jnp.clip(result, -reach, reach).astype(kind)


def setup_inputs(seed: int = 0) -> dict:
    key_list = jax.random.split(jax.random.key(seed), 9)
    tokens = normal_values(key_list[0], (TOKENS, D), 1.0, 6.0, ((0, 512),))
    route_ids_keys = jax.random.split(jax.random.fold_in(key_list[1], 1), TOKENS // TOK_DEV)
    route_ids_turns = jax.random.permutation(jax.random.fold_in(key_list[1], 3), TOKENS // TOK_DEV)
    route_ids = jax.vmap(lambda own, number: deal_out(jax.random.fold_in(key_list[1], 2), own, number, TOK_DEV, EXPERTS, TOP, CAPE, 2))(route_ids_keys, route_ids_turns).reshape((TOKENS, TOP))
    gate_weights = jnp.clip(0.05 + 0.25 * jax.random.uniform(key_list[2], (TOKENS, TOP), jnp.float32) ** levels(key_list[2], (TOKENS, TOP), ((0, 512),), -0.2, 0.2), 0.05, 0.3)
    tenant_ids = plant(jax.random.randint(key_list[3], (TOKENS,), 0, TEN), jax.random.fold_in(key_list[3], 1), 0, TEN - 1).astype(jnp.int32)
    up_weight = normal_values(key_list[4], (EXPERTS, D, F), D ** -0.5, 0.09375, ((0, 64), (1, 8)))
    down_weight = normal_values(key_list[5], (EXPERTS, F, D), F ** -0.5, 0.1875, ((0, 64), (2, 8)))
    adapter_in = normal_values(key_list[6], (EXPERTS, D, TEN * RANK), D ** -0.5, 0.09375, ((0, 64), (1, 8)))
    adapter_out = normal_values(key_list[7], (EXPERTS, TEN * RANK, F), RANK ** -0.5, 1.5, ((0, 64),))
    return {"tokens": tokens, "route_ids": route_ids, "gate_weights": gate_weights, "tenant_ids": tenant_ids, "up_weight": up_weight, "down_weight": down_weight, "adapter_in": adapter_in, "adapter_out": adapter_out}


def reference(tokens, route_ids, gate_weights, tenant_ids, up_weight, down_weight, adapter_in, adapter_out):
    total = tokens.shape[0]
    devices = total // TOK_DEV
    per_dev = TOK_DEV * TOP
    flat_routes = route_ids.reshape(devices, per_dev)
    same = flat_routes[:, :, None] == flat_routes[:, None, :]
    order = jnp.arange(per_dev, dtype=jnp.int32)
    earlier = order[None, :] < order[:, None]
    rank = jnp.sum((same & earlier[None]).astype(jnp.int32), axis=2).astype(jnp.int32)
    device_ids = jnp.arange(devices, dtype=jnp.int32)[:, None]
    position = (device_ids * CAPE + rank).reshape(-1).astype(jnp.int32)
    expert_of = flat_routes.reshape(-1).astype(jnp.int32)
    token_of = jnp.repeat(jnp.arange(total, dtype=jnp.int32), TOP)
    depth = devices * CAPE
    slot_index = (expert_of * depth + position).astype(jnp.int32)
    table = jnp.full((EXPERTS * depth,), -1, jnp.int32).at[slot_index].set(token_of)
    piece = D // N_DP
    columns = jnp.arange(TEN * RANK, dtype=jnp.int32) // RANK

    def one_expert(args):
        rows, w_up, w_down, a_in, adapter_expand_output = args
        live = rows >= 0
        safe = jnp.maximum(rows, 0).astype(jnp.int32)
        gathered = jnp.where(live[:, None], tokens[safe], jnp.zeros((), tokens.dtype))
        blocks = gathered.reshape(depth, N_DP, piece).astype(jnp.float32)
        up_parts = jnp.einsum('spd,pdf->spf', blocks, w_up.reshape(N_DP, piece, F).astype(jnp.float32))
        up_projected = jnp.sum(up_parts.astype(jnp.bfloat16).astype(jnp.float32), axis=1)
        shrink_parts = jnp.einsum('spd,pdr->spr', blocks, a_in.reshape(N_DP, piece, TEN * RANK).astype(jnp.float32))
        shrink = jnp.sum(shrink_parts.astype(jnp.bfloat16).astype(jnp.float32), axis=1)
        tenant = jnp.where(live, tenant_ids[safe], -1)
        keep = columns[None, :] == tenant[:, None]
        masked_values = jnp.where(keep, shrink, jnp.zeros((), jnp.float32))
        low_rank_adapter = jnp.dot(masked_values, adapter_expand_output.astype(jnp.float32), precision=lax.Precision.HIGHEST)
        hidden_activations = jax.nn.silu(up_projected + low_rank_adapter).astype(jnp.bfloat16)
        return jnp.dot(hidden_activations, w_down, preferred_element_type=jnp.float32).astype(jnp.bfloat16)

    outputs = lax.map(one_expert, (table.reshape(EXPERTS, depth), up_weight, down_weight, adapter_in, adapter_out))
    results = outputs.reshape(EXPERTS * depth, D)
    slots_grid = slot_index.reshape(total, TOP)

    def add_choice(acc, k):
        picked = results[slots_grid[:, k]].astype(jnp.float32)
        return acc + picked * gate_weights[:, k][:, None], None

    mixed, _ = lax.scan(add_choice, jnp.zeros((total, D), jnp.float32), jnp.arange(TOP, dtype=jnp.int32))
    return mixed.astype(jnp.bfloat16)
```

```python
import functools
import jax
import jax.numpy as jnp
from jax import lax
from jax.experimental import pallas as pl
from jax.experimental.pallas import tpu as pltpu
from jax.sharding import Mesh, PartitionSpec as P

BF = jnp.bfloat16
F32 = jnp.float32
TOK = 16
TOP = 8
PLANE = 8
TEN = 4
RANK = 16
WIDE = 1024
META = 128
ROUTE_AT = 64
GATE_AT = 72
GROUP = 256


def _matches(meta, z):
    lane = lax.broadcasted_iota(jnp.int32, (GROUP, META), 1)
    expert = jnp.where(lane < PLANE, lane + z * PLANE, -1).astype(F32)
    return [meta[:, ROUTE_AT + k : ROUTE_AT + k + 1] == expert for k in range(TOP)]


def _slots(matches):
    named = sum(m.astype(F32) for m in matches)
    row = lax.broadcasted_iota(jnp.int32, (GROUP, GROUP), 0)
    col = lax.broadcasted_iota(jnp.int32, (GROUP, GROUP), 1)
    before = ((row // TOK == col // TOK) & (col < row)).astype(BF)
    rank = jnp.dot(before, named.astype(BF), preferred_element_type=F32)
    seat = named * (rank + 1.0)
    spread = _spread()
    at = jnp.dot(seat.astype(BF), spread, preferred_element_type=F32)
    want = (col % 2 + 1).astype(F32)
    return (at == want) & (row // TOK == (col % 32) // 2)


def _spread():
    e = lax.broadcasted_iota(jnp.int32, (META, GROUP), 0)
    j = lax.broadcasted_iota(jnp.int32, (META, GROUP), 1)
    return (e == j // 32).astype(BF)


def _select_kernel(z_ref, t_ref, o_ref):
    t = t_ref[...].reshape(GROUP, WIDE + META)
    slots = _slots(_matches(t[:, WIDE:].astype(F32), z_ref[0])).astype(BF)
    out = lax.dot_general(slots, t, (((0,), (0,)), ((), ())), preferred_element_type=F32)
    o_ref[...] = out.astype(BF).reshape(PLANE, 32, WIDE + META)


def _select(z, table):
    return pl.pallas_call(
        _select_kernel,
        grid_spec=pltpu.PrefetchScalarGridSpec(
            num_scalar_prefetch=1,
            grid=(4,),
            in_specs=[pl.BlockSpec((4, 64, WIDE + META), lambda g, z: (g, 0, 0))],
            out_specs=pl.BlockSpec((PLANE, 32, WIDE + META), lambda g, z: (0, g, 0)),
        ),
        out_shape=jax.ShapeDtypeStruct((PLANE, 128, WIDE + META), BF),
        compiler_params=pltpu.CompilerParams(vmem_limit_bytes=32 << 20),
        name="select",
    )(z, table)


def _up_kernel(x_ref, w_ref, o_ref):
    acc = jnp.dot(x_ref[:, :WIDE], w_ref[...], preferred_element_type=F32)
    o_ref[:, :WIDE] = acc[:, :WIDE].astype(BF)
    o_ref[:, WIDE:] = (acc[:, WIDE:] * x_ref[:, WIDE:].astype(F32)).astype(BF)


def _up(x, w):
    rows = x.shape[0]
    return pl.pallas_call(
        _up_kernel,
        grid=(rows // 256,),
        in_specs=[
            pl.BlockSpec((256, WIDE + META), lambda g: (g, 0)),
            pl.BlockSpec((WIDE, WIDE + META), lambda g: (0, 0)),
        ],
        out_specs=pl.BlockSpec((256, WIDE + META), lambda g: (g, 0)),
        out_shape=jax.ShapeDtypeStruct((rows, WIDE + META), BF),
        compiler_params=pltpu.CompilerParams(vmem_limit_bytes=32 << 20),
        name="up",
    )(x, w)


def _act_kernel(c_ref, u_ref, a_ref, o_ref):
    lora = jnp.dot(u_ref[:, WIDE : WIDE + 64], a_ref[0], preferred_element_type=F32)
    v = u_ref[:, :WIDE].astype(F32) + lora
    o_ref[...] = (v / (1.0 + jnp.exp(-v))).astype(BF)


def _act(c, u, adapter_out):
    rows = u.shape[0]
    return pl.pallas_call(
        _act_kernel,
        grid_spec=pltpu.PrefetchScalarGridSpec(
            num_scalar_prefetch=1,
            grid=(rows // 128,),
            in_specs=[
                pl.BlockSpec((128, WIDE + META), lambda g, c: (g, 0)),
                pl.BlockSpec((1, 64, WIDE), lambda g, c: (c[0], 0, 0)),
            ],
            out_specs=pl.BlockSpec((128, WIDE), lambda g, c: (g, 0)),
        ),
        out_shape=jax.ShapeDtypeStruct((rows, WIDE), BF),
        compiler_params=pltpu.CompilerParams(vmem_limit_bytes=32 << 20),
        name="act",
    )(c, u, adapter_out)


def _down_kernel(x_ref, w_ref, o_ref):
    o_ref[...] = jnp.dot(x_ref[...], w_ref[...], preferred_element_type=F32).astype(BF)


def _down(x, w):
    rows = x.shape[0]
    return pl.pallas_call(
        _down_kernel,
        grid=(rows // 256,),
        in_specs=[
            pl.BlockSpec((256, WIDE), lambda g: (g, 0)),
            pl.BlockSpec((WIDE, WIDE), lambda g: (0, 0)),
        ],
        out_specs=pl.BlockSpec((256, WIDE), lambda g: (g, 0)),
        out_shape=jax.ShapeDtypeStruct((rows, WIDE), BF),
        compiler_params=pltpu.CompilerParams(vmem_limit_bytes=32 << 20),
        name="down",
    )(x, w)


def _combine_kernel(z_ref, m_ref, y_ref, o_ref):
    meta = m_ref[...].reshape(GROUP, META).astype(F32)
    matches = _matches(meta, z_ref[0])
    gate = sum(jnp.where(m, meta[:, GATE_AT + k : GATE_AT + k + 1], 0.0) for k, m in enumerate(matches))
    gates = jnp.dot(gate.astype(BF), _spread(), preferred_element_type=F32)
    weight = jnp.where(_slots(matches), gates, 0.0).astype(BF)
    out = jnp.dot(weight, y_ref[...].reshape(GROUP, WIDE), preferred_element_type=F32)
    o_ref[...] = out.astype(BF).reshape(4, 64, WIDE)


def _combine(z, table, back):
    return pl.pallas_call(
        _combine_kernel,
        grid_spec=pltpu.PrefetchScalarGridSpec(
            num_scalar_prefetch=1,
            grid=(4,),
            in_specs=[
                pl.BlockSpec((4, 64, META), lambda g, z: (g, 0, WIDE // META)),
                pl.BlockSpec((PLANE, 32, WIDE), lambda g, z: (0, g, 0)),
            ],
            out_specs=pl.BlockSpec((4, 64, WIDE), lambda g, z: (g, 0, 0)),
        ),
        out_shape=jax.ShapeDtypeStruct((16, 64, WIDE), BF),
        compiler_params=pltpu.CompilerParams(vmem_limit_bytes=32 << 20),
        name="combine",
    )(z, table, back)


def per_device(tokens, route_ids, gate_weights, tenant_ids, up_weight, down_weight, adapter_in, adapter_out):
    z = lax.axis_index("z").astype(jnp.int32).reshape(1)
    core = lax.axis_index("core").astype(jnp.int32)

    def both(w, axis):
        own = lax.dynamic_index_in_dim(w, core, 0, keepdims=False)
        other = lax.dynamic_index_in_dim(w, 1 - core, 0, keepdims=False)
        other = lax.ppermute(other, "core", [(0, 1), (1, 0)])
        first = jnp.where(core == 0, own, other)
        second = jnp.where(core == 0, other, own)
        return jnp.concatenate([first, second], axis=axis)

    w_up = both(up_weight, 0)
    w_in = both(adapter_in, 0)
    w_down = both(down_weight, 1)
    w_cat = jnp.concatenate([w_up, w_in, jnp.zeros((WIDE, META - TEN * RANK), BF)], axis=1)

    owner = jnp.arange(TEN * RANK, dtype=jnp.int32) // RANK
    mask = (owner[None, :] == tenant_ids[:, None]).astype(BF)
    meta = jnp.concatenate(
        [mask, route_ids.astype(BF), gate_weights.astype(BF), jnp.zeros((TOK, META - 80), BF)], axis=1
    )
    pieces = tokens.reshape(TOK, 4, WIDE).transpose(1, 0, 2)
    rows = jnp.concatenate([pieces, jnp.broadcast_to(meta[None], (4, TOK, META))], axis=2)
    mine = lax.all_to_all(rows, "x", 0, 0, tiled=True).reshape(64, WIDE + META)
    table = lax.all_gather(mine, "z", axis=0)
    sending = _select(z, table)
    arrived = lax.all_to_all(sending, ("y", "core"), 0, 0, tiled=True).reshape(1024, WIDE + META)
    part = _up(arrived, w_cat)
    summed = lax.psum_scatter(part, "x", scatter_dimension=0, tiled=True)
    hidden_part = _act(core.reshape(1), summed, adapter_out)
    hidden = lax.all_gather(hidden_part, "x", axis=0, tiled=True)
    out = _down(hidden, w_down).reshape(8, 128, WIDE)
    back = lax.all_to_all(out, ("y", "core"), 0, 0, tiled=True)
    partial = _combine(z, table, back).reshape(1024, WIDE)
    mixed = lax.psum_scatter(partial, "z", scatter_dimension=0, tiled=True)
    home = lax.all_to_all(mixed.reshape(4, TOK, WIDE), "x", 0, 0, tiled=True)
    return home.transpose(1, 0, 2).reshape(TOK, 4 * WIDE)


def solution(mesh):
    fine = Mesh(mesh.devices.reshape(4, 2, 16, 4), ("x", "core", "z", "y"))
    dp, ex = ("x", "core"), ("z", "y")
    every = dp + ex
    placed = (
        P(every, None),
        P(every, None),
        P(every, None),
        P(every),
        P(ex, dp, None),
        P(ex, None, dp),
        P(ex, dp, None),
        P(ex, None, None),
    )
    return jax.shard_map(per_device, mesh=fine, in_specs=placed, out_specs=P(every, None), check_vma=False)
```

```python
import jax
import jax.numpy as jnp
from jax import lax
from jax.experimental import pallas as pl
from jax.experimental.pallas import tpu as pltpu
from jax.sharding import Mesh, PartitionSpec as P

BF = jnp.bfloat16
F32 = jnp.float32
TOK = 16
TOP = 8
PLANE = 8
TEN = 4
RANK = 16
WIDE = 1024
META = 128
ROUTE_AT = 64
GATE_AT = 72
GROUP = 256
F16 = jnp.float16
PARAMS = pltpu.CompilerParams(vmem_limit_bytes=24 << 20)


def _matches(meta, z):
    lane = lax.broadcasted_iota(jnp.int32, (GROUP, META), 1)
    expert = jnp.where(lane < PLANE, lane + z * PLANE, -1).astype(F32)
    return [meta[:, ROUTE_AT + k : ROUTE_AT + k + 1] == expert for k in range(TOP)]


def _slots(matches):
    named = sum(m.astype(F32) for m in matches)
    row = lax.broadcasted_iota(jnp.int32, (GROUP, GROUP), 0)
    col = lax.broadcasted_iota(jnp.int32, (GROUP, GROUP), 1)
    before = ((row // TOK == col // TOK) & (col < row)).astype(BF)
    rank = jnp.dot(before, named.astype(BF), preferred_element_type=F32)
    seat = named * (rank + 1.0)
    spread = _spread()
    at = jnp.dot(seat.astype(BF), spread, preferred_element_type=F32)
    want = (col % 2 + 1).astype(F32)
    return (at == want) & (row // TOK == (col % 32) // 2)


def _spread():
    e = lax.broadcasted_iota(jnp.int32, (META, GROUP), 0)
    j = lax.broadcasted_iota(jnp.int32, (META, GROUP), 1)
    return (e == j // 32).astype(BF)


def _whole(after):
    return [pl.BlockSpec(memory_space=pl.ANY) for _ in after]


def _select_kernel(z_ref, t_ref, *rest):
    o_ref = rest[-1]
    t = t_ref[...].reshape(GROUP, WIDE + META)
    slots = _slots(_matches(t[:, WIDE:].astype(F32), z_ref[0])).astype(BF)
    out = lax.dot_general(slots, t, (((0,), (0,)), ((), ())), preferred_element_type=F32)
    o_ref[...] = out.astype(BF).reshape(PLANE, 32, WIDE + META)


def _select(z, table, half, after=()):
    return pl.pallas_call(
        _select_kernel,
        grid_spec=pltpu.PrefetchScalarGridSpec(
            num_scalar_prefetch=1,
            grid=(2,),
            in_specs=[pl.BlockSpec((8, 32, WIDE + META), lambda g, z: (g, half, 0))] + _whole(after),
            out_specs=pl.BlockSpec((PLANE, 32, WIDE + META), lambda g, z: (0, g, 0)),
        ),
        out_shape=jax.ShapeDtypeStruct((PLANE, 64, WIDE + META), BF),
        compiler_params=PARAMS,
        name="select",
    )(z, table, *after)


def _up_kernel(c_ref, x_own, x_other, mask, w_own, w_other, a_own, a_other, *rest):
    o_ref = rest[-1]
    up = jnp.dot(x_own[...], w_own[0], preferred_element_type=F32)
    up += jnp.dot(x_other[...], w_other[...], preferred_element_type=F32)
    o_ref[:, :WIDE] = up.astype(BF)
    shrink = jnp.dot(x_own[...], a_own[0], preferred_element_type=F32)
    shrink += jnp.dot(x_other[...], a_other[...], preferred_element_type=F32)
    shrink *= mask[:, :64].astype(F32)
    o_ref[:, WIDE:] = jnp.concatenate([shrink, jnp.zeros_like(shrink)], axis=1).astype(BF)


def _up(c, x, w, w_other, a, a_other, after=()):
    rows = x.shape[0]
    step = 256
    return pl.pallas_call(
        _up_kernel,
        grid_spec=pltpu.PrefetchScalarGridSpec(
            num_scalar_prefetch=1,
            grid=(rows // step,),
            in_specs=[
                pl.BlockSpec((step, 512), lambda g, c: (g, c[0])),
                pl.BlockSpec((step, 512), lambda g, c: (g, 1 - c[0])),
                pl.BlockSpec((step, META), lambda g, c: (g, WIDE // META)),
                pl.BlockSpec((1, 512, WIDE), lambda g, c: (c[0], 0, 0)),
                pl.BlockSpec((512, WIDE), lambda g, c: (0, 0)),
                pl.BlockSpec((1, 512, 64), lambda g, c: (c[0], 0, 0)),
                pl.BlockSpec((512, 64), lambda g, c: (0, 0)),
            ]
            + _whole(after),
            out_specs=pl.BlockSpec((step, WIDE + META), lambda g, c: (g, 0)),
        ),
        out_shape=jax.ShapeDtypeStruct((rows, WIDE + META), BF),
        compiler_params=PARAMS,
        name="up",
    )(c, x, x, x, w, w_other, a, a_other, *after)


def _act_kernel(c_ref, u_ref, a_ref, o_ref):
    lora = jnp.dot(u_ref[:, WIDE : WIDE + 64], a_ref[0], preferred_element_type=F32)
    v = u_ref[:, :WIDE].astype(F32) + lora
    o_ref[...] = (v / (1.0 + jnp.exp(-v))).astype(BF)


def _act(c, u, adapter_out):
    rows = u.shape[0]
    step = 64
    return pl.pallas_call(
        _act_kernel,
        grid_spec=pltpu.PrefetchScalarGridSpec(
            num_scalar_prefetch=1,
            grid=(rows // step,),
            in_specs=[
                pl.BlockSpec((step, WIDE + META), lambda g, c: (g, 0)),
                pl.BlockSpec((1, 64, WIDE), lambda g, c: (c[0], 0, 0)),
            ],
            out_specs=pl.BlockSpec((step, WIDE), lambda g, c: (g, 0)),
        ),
        out_shape=jax.ShapeDtypeStruct((rows, WIDE), BF),
        compiler_params=PARAMS,
        name="act",
    )(c, u, adapter_out)


def _down_kernel(at, own, left, right, far_low, far_high, w_own, w_other, o_ref):
    g = pl.program_id(0)
    core = at[0]

    def run(h):
        for side, w in ((core, w_own[0]), (1 - core, w_other[...])):
            cols = pl.ds(pl.multiple_of(side * 512, 512), 512)
            o_ref[:, cols] = jnp.dot(h, w, preferred_element_type=F32).astype(BF)

    @pl.when(g == 0)
    def _():
        run(own[...])

    @pl.when(g == 1)
    def _():
        run(left[...])

    @pl.when(g == 2)
    def _():
        run(right[...])

    @pl.when(g == 3)
    def _():
        run(jnp.concatenate([far_low[...], far_high[...]], axis=0))


def _down(at, parts, w, w_other):
    rows = parts[0].shape[0]
    place = (0, 3, 1, 2)

    def target(g, at):
        off = jnp.where(g == 0, place[0], jnp.where(g == 1, place[1], jnp.where(g == 2, place[2], place[3])))
        return (lax.rem(at[1] + off, 4), 0)

    return pl.pallas_call(
        _down_kernel,
        grid_spec=pltpu.PrefetchScalarGridSpec(
            num_scalar_prefetch=1,
            grid=(4,),
            in_specs=[pl.BlockSpec(p.shape, lambda g, at: (0, 0)) for p in parts]
            + [
                pl.BlockSpec((1, WIDE, 512), lambda g, at: (at[0], 0, 0)),
                pl.BlockSpec((WIDE, 512), lambda g, at: (0, 0)),
            ],
            out_specs=pl.BlockSpec((rows, WIDE), target),
        ),
        out_shape=jax.ShapeDtypeStruct((4 * rows, WIDE), BF),
        compiler_params=PARAMS,
        name="down",
    )(at, *parts, w, w_other)


def _combine_kernel(z_ref, m_ref, y_ref, *rest):
    o_ref = rest[-1]
    meta = m_ref[...].reshape(GROUP, META).astype(F32)
    matches = _matches(meta, z_ref[0])
    gate = sum(jnp.where(m, meta[:, GATE_AT + k : GATE_AT + k + 1], 0.0) for k, m in enumerate(matches))
    gates = jnp.dot(gate.astype(BF), _spread(), preferred_element_type=F32)
    weight = jnp.where(_slots(matches), gates, 0.0).astype(BF)
    out = jnp.dot(weight, y_ref[...].reshape(GROUP, WIDE), preferred_element_type=F32)
    o_ref[...] = out.astype(BF).reshape(8, 32, WIDE)


def _combine(z, table, back, half, after=()):
    return pl.pallas_call(
        _combine_kernel,
        grid_spec=pltpu.PrefetchScalarGridSpec(
            num_scalar_prefetch=1,
            grid=(2,),
            in_specs=[
                pl.BlockSpec((8, 32, META), lambda g, z: (g, half, WIDE // META)),
                pl.BlockSpec((PLANE, 32, WIDE), lambda g, z: (0, g, 0)),
            ]
            + _whole(after),
            out_specs=pl.BlockSpec((8, 32, WIDE), lambda g, z: (g, 0, 0)),
        ),
        out_shape=jax.ShapeDtypeStruct((16, 32, WIDE), BF),
        compiler_params=PARAMS,
        name="combine",
    )(z, table, back, *after)


def _total_kernel(p_ref, *rest):
    o_ref = rest[-1]
    o_ref[...] = jnp.sum(p_ref[...].astype(F32), axis=0).astype(BF)


def _total(p, after=()):
    n, rows, wide = p.shape
    return pl.pallas_call(
        _total_kernel,
        grid=(2,),
        in_specs=[pl.BlockSpec((n, rows // 2, wide), lambda g: (0, g, 0))] + _whole(after),
        out_specs=pl.BlockSpec((rows // 2, wide), lambda g: (g, 0)),
        out_shape=jax.ShapeDtypeStruct((rows, wide), BF),
        compiler_params=PARAMS,
        name="total",
    )(p, *after)


def _shift(v, axis, size, by):
    return lax.ppermute(v, axis, [(i, (i + by) % size) for i in range(size)])


def _gather_x(h):
    k = h.shape[0] // 2
    left, right = _shift(h, "x", 4, 1), _shift(h, "x", 4, -1)
    return [h, left, right, _shift(left[:k], "x", 4, 1), _shift(right[k:], "x", 4, -1)]


def per_device(tokens, route_ids, gate_weights, tenant_ids, up_weight, down_weight, adapter_in, adapter_out):
    z = lax.axis_index("z").astype(jnp.int32).reshape(1)
    core = lax.axis_index("core").astype(jnp.int32)
    c = core.reshape(1)
    at = jnp.stack([core, lax.axis_index("x").astype(jnp.int32)])

    def swapped(w):
        return _shift(lax.dynamic_index_in_dim(w, 1 - core, 0, keepdims=False), "core", 2, 1)

    owner = jnp.arange(TEN * RANK, dtype=jnp.int32) // RANK
    mask = (owner[None, :] == tenant_ids[:, None]).astype(BF)
    meta = jnp.concatenate(
        [mask, route_ids.astype(BF), gate_weights.astype(BF), jnp.zeros((TOK, META - 80), BF)], axis=1
    )
    pieces = tokens.reshape(TOK, 4, WIDE).transpose(1, 0, 2)
    rows = jnp.concatenate([pieces, jnp.broadcast_to(meta[None], (4, TOK, META))], axis=2)
    mine = lax.all_to_all(rows, "x", 0, 0, tiled=True).reshape(64, WIDE + META)
    table = lax.all_gather(mine.astype(F16), "z", axis=0).astype(BF)

    up_other, in_other, down_other = swapped(up_weight), swapped(adapter_in), swapped(down_weight)
    halves = (0, 1)
    sending, part, back = [], [], []
    for h in (0, 1):
        sending.append(_select(z, table, h, sending[-1:]))
    for h in (0, 1):
        arrived = lax.all_to_all(sending[h], ("y", "core"), 0, 0, tiled=True).reshape(512, WIDE + META)
        part.append(_up(c, arrived, up_weight, up_other, adapter_in, in_other, part[-1:]))
    for h in (0, 1):
        summed = lax.psum_scatter(part[h], "x", scatter_dimension=0, tiled=True)
        hidden = _gather_x(_act(c, summed, adapter_out))
        out = _down(at, hidden, down_weight, down_other).reshape(8, 64, WIDE)
        back.append(lax.all_to_all(out, ("y", "core"), 0, 0, tiled=True))
    plane, total = [], []
    for h in (0, 1):
        plane.append(_combine(z, table, back[h], h, plane[-1:]))
    for h in (0, 1):
        total.append(_total(lax.all_to_all(plane[h], "z", 0, 0, tiled=True), total[-1:]))
    mixed = jnp.concatenate(total, axis=0)
    home = lax.all_to_all(mixed.reshape(4, TOK, WIDE), "x", 0, 0, tiled=True)
    return home.transpose(1, 0, 2).reshape(TOK, 4 * WIDE)


def solution(mesh):
    fine = Mesh(mesh.devices.reshape(4, 2, 16, 4), ("x", "core", "z", "y"))
    dp, ex = ("x", "core"), ("z", "y")
    every = dp + ex
    placed = (
        P(every, None),
        P(every, None),
        P(every, None),
        P(every),
        P(ex, dp, None),
        P(ex, None, dp),
        P(ex, dp, None),
        P(ex, None, None),
    )
    return jax.shard_map(per_device, mesh=fine, in_specs=placed, out_specs=P(every, None), check_vma=False)
```

```python
import jax
import jax.numpy as jnp
from jax import lax
from jax.experimental import pallas as pl
from jax.experimental.pallas import tpu as pltpu
from jax.sharding import Mesh, PartitionSpec as P

BF = jnp.bfloat16
F16 = jnp.float16
F32 = jnp.float32
TOK = 16
TOP = 8
PLANE = 8
TEN = 4
RANK = 16
PIECE = 1024
WIDE = 4096
META = 128
ROUTE_AT = 64
GATE_AT = 72
GROUP = 256
AROUND = (0, 3, 1, 2)


def _matches(meta, z):
    lane = lax.broadcasted_iota(jnp.int32, (GROUP, META), 1)
    expert = jnp.where(lane < PLANE, lane + z * PLANE, -1).astype(F32)
    return [meta[:, ROUTE_AT + k : ROUTE_AT + k + 1] == expert for k in range(TOP)]


def _slots(matches):
    named = sum(m.astype(F32) for m in matches)
    row = lax.broadcasted_iota(jnp.int32, (GROUP, GROUP), 0)
    col = lax.broadcasted_iota(jnp.int32, (GROUP, GROUP), 1)
    before = ((row // TOK == col // TOK) & (col < row)).astype(BF)
    rank = jnp.dot(before, named.astype(BF), preferred_element_type=F32)
    seat = named * (rank + 1.0)
    spread = _spread()
    at = jnp.dot(seat.astype(BF), spread, preferred_element_type=F32)
    want = (col % 2 + 1).astype(F32)
    return (at == want) & (row // TOK == (col % 32) // 2)


def _spread():
    e = lax.broadcasted_iota(jnp.int32, (META, GROUP), 0)
    j = lax.broadcasted_iota(jnp.int32, (META, GROUP), 1)
    return (e == j // 32).astype(BF)


def _params(mib):
    return pltpu.CompilerParams(vmem_limit_bytes=mib << 20)


def _piece(g, x):
    off = jnp.where(g == 0, AROUND[0], jnp.where(g == 1, AROUND[1], jnp.where(g == 2, AROUND[2], AROUND[3])))
    return lax.rem(x + off, 4)


def _select_kernel(z_ref, m_ref, t_ref, o_ref):
    slots = _slots(_matches(m_ref[...].reshape(GROUP, META).astype(F32), z_ref[0])).astype(BF)
    t = t_ref[...].reshape(GROUP, t_ref.shape[2])
    out = lax.dot_general(slots, t, (((0,), (0,)), ((), ())), preferred_element_type=F32)
    o_ref[...] = out.astype(BF).reshape(o_ref.shape)


def _select(z, table):
    width = (WIDE + META) // 3
    return pl.pallas_call(
        _select_kernel,
        grid_spec=pltpu.PrefetchScalarGridSpec(
            num_scalar_prefetch=1,
            grid=(3,),
            in_specs=[
                pl.BlockSpec((16, TOK, META), lambda g, z: (0, 0, WIDE // META)),
                pl.BlockSpec((16, TOK, width), lambda g, z: (0, 0, g)),
            ],
            out_specs=pl.BlockSpec((PLANE, 32, width), lambda g, z: (0, 0, g)),
        ),
        out_shape=jax.ShapeDtypeStruct((PLANE, 32, WIDE + META), BF),
        compiler_params=_params(24),
        name="select",
    )(z, table, table)


def _up_kernel(at, x_ref, m_ref, own, left, right, far_low, far_high, a_in, a_out, o_ref, acc, shrink):
    g = pl.program_id(0)

    def add(w):
        acc[...] += jnp.dot(x_ref[...], w, preferred_element_type=F32)

    @pl.when(g == 0)
    def _():
        acc[...] = jnp.dot(x_ref[...], own[...], preferred_element_type=F32)
        shrink[...] = jnp.zeros_like(shrink)

    @pl.when(g == 1)
    def _():
        add(left[...])

    @pl.when(g == 2)
    def _():
        add(right[...])

    shrink[...] += jnp.dot(x_ref[...], a_in[...], preferred_element_type=F32)

    @pl.when(g == 3)
    def _():
        acc[...] += jnp.dot(x_ref[:, :512], far_low[...], preferred_element_type=F32)
        acc[...] += jnp.dot(x_ref[:, 512:], far_high[...], preferred_element_type=F32)
        kept = shrink[...] * m_ref[:, :64].astype(F32)
        high = kept.astype(BF)
        low = (kept - high.astype(F32)).astype(BF)
        v = acc[...] + jnp.dot(high, a_out[0], preferred_element_type=F32)
        v += jnp.dot(low, a_out[0], preferred_element_type=F32)
        o_ref[...] = (v / (1.0 + jnp.exp(-v))).astype(BF)


def _up(at, rows, w, a_in, a_out):
    full = lambda p: pl.BlockSpec(p.shape, lambda g, at: (0, 0))
    return pl.pallas_call(
        _up_kernel,
        grid_spec=pltpu.PrefetchScalarGridSpec(
            num_scalar_prefetch=1,
            grid=(4,),
            in_specs=[
                pl.BlockSpec((GROUP, PIECE), lambda g, at: (0, _piece(g, at[1]))),
                pl.BlockSpec((GROUP, META), lambda g, at: (0, WIDE // META)),
            ]
            + [full(p) for p in w]
            + [
                pl.BlockSpec((PIECE, 64), lambda g, at: (_piece(g, at[1]), 0)),
                pl.BlockSpec((1, 64, PIECE), lambda g, at: (at[0], 0, 0)),
            ],
            out_specs=pl.BlockSpec((GROUP, PIECE), lambda g, at: (0, 0)),
            scratch_shapes=[pltpu.VMEM((GROUP, PIECE), F32), pltpu.VMEM((GROUP, 64), F32)],
        ),
        out_shape=jax.ShapeDtypeStruct((GROUP, PIECE), BF),
        compiler_params=_params(32),
        name="up",
    )(at, rows, rows, *w, a_in, a_out)


def _down_kernel(at, h_ref, own, left, right, far_low, far_high, o_ref):
    g = pl.program_id(0)
    for i, w in enumerate((own, left, right)):

        @pl.when(g == i)
        def _():
            o_ref[...] = jnp.dot(h_ref[...], w[...], preferred_element_type=F32).astype(BF)

    @pl.when(g == 3)
    def _():
        out = jnp.dot(h_ref[:, :512], far_low[...], preferred_element_type=F32)
        out += jnp.dot(h_ref[:, 512:], far_high[...], preferred_element_type=F32)
        o_ref[...] = out.astype(BF)


def _down(at, hidden, w):
    full = lambda p: pl.BlockSpec(p.shape, lambda g, at: (0, 0))
    return pl.pallas_call(
        _down_kernel,
        grid_spec=pltpu.PrefetchScalarGridSpec(
            num_scalar_prefetch=1,
            grid=(4,),
            in_specs=[full(hidden)] + [full(p) for p in w],
            out_specs=pl.BlockSpec((GROUP, PIECE), lambda g, at: (0, _piece(g, at[1]))),
        ),
        out_shape=jax.ShapeDtypeStruct((GROUP, WIDE), BF),
        compiler_params=_params(32),
        name="down",
    )(at, hidden, *w)


def _combine_kernel(z_ref, m_ref, y_ref, o_ref, weight):
    @pl.when(pl.program_id(0) == 0)
    def _():
        meta = m_ref[...].reshape(GROUP, META).astype(F32)
        matches = _matches(meta, z_ref[0])
        gate = sum(jnp.where(m, meta[:, GATE_AT + k : GATE_AT + k + 1], 0.0) for k, m in enumerate(matches))
        gates = jnp.dot(gate.astype(BF), _spread(), preferred_element_type=F32)
        weight[...] = jnp.where(_slots(matches), gates, 0.0).astype(BF)

    out = jnp.dot(weight[...], y_ref[...].reshape(GROUP, PIECE), preferred_element_type=F32)
    o_ref[...] = out.astype(BF)


def _combine(z, table, back):
    return pl.pallas_call(
        _combine_kernel,
        grid_spec=pltpu.PrefetchScalarGridSpec(
            num_scalar_prefetch=1,
            grid=(4,),
            in_specs=[
                pl.BlockSpec((16, TOK, META), lambda g, z: (0, 0, WIDE // META)),
                pl.BlockSpec((PLANE, 32, PIECE), lambda g, z: (0, 0, g)),
            ],
            out_specs=pl.BlockSpec((GROUP, PIECE), lambda g, z: (0, g)),
            scratch_shapes=[pltpu.VMEM((GROUP, GROUP), BF)],
        ),
        out_shape=jax.ShapeDtypeStruct((GROUP, WIDE), BF),
        compiler_params=_params(24),
        name="combine",
    )(z, table, back)


def _shift(v, axis, size, by):
    return lax.ppermute(v, axis, [(i, (i + by) % size) for i in range(size)])


def _gather_x(w):
    left, right = _shift(w, "x", 4, 1), _shift(w, "x", 4, -1)
    return [w, left, right, _shift(left[:512], "x", 4, 1), _shift(right[512:], "x", 4, -1)]


def per_device(tokens, route_ids, gate_weights, tenant_ids, up_weight, down_weight, adapter_in, adapter_out):
    z = lax.axis_index("z").astype(jnp.int32).reshape(1)
    core = lax.axis_index("core").astype(jnp.int32)
    at = jnp.stack([core, lax.axis_index("x").astype(jnp.int32)])

    def both(w, axis):
        own = lax.dynamic_index_in_dim(w, core, 0, keepdims=False)
        other = _shift(lax.dynamic_index_in_dim(w, 1 - core, 0, keepdims=False), "core", 2, 1)
        first, second = jnp.where(core == 0, own, other), jnp.where(core == 0, other, own)
        return jnp.concatenate([first, second], axis=axis)

    w_up = _gather_x(both(up_weight, 0))
    w_down = _gather_x(both(down_weight, 1))
    a_in = lax.dynamic_index_in_dim(lax.all_gather(adapter_in, ("x", "core"), axis=1, tiled=True), core, 0, keepdims=False)

    owner = jnp.arange(TEN * RANK, dtype=jnp.int32) // RANK
    mask = (owner[None, :] == tenant_ids[:, None]).astype(F16)
    meta = jnp.concatenate(
        [mask, route_ids.astype(F16), gate_weights.astype(F16), jnp.zeros((TOK, META - 80), F16)], axis=1
    )
    mine = jnp.concatenate([tokens.astype(F16), meta], axis=1)
    table = lax.all_gather(mine, "z", axis=0).astype(BF)
    sending = _select(z, table)
    arrived = lax.all_to_all(sending, ("y", "core"), 0, 0, tiled=True).reshape(GROUP, WIDE + META)
    hidden = _up(at, arrived, w_up, a_in, adapter_out)
    out = _down(at, hidden, w_down).reshape(PLANE, 32, WIDE)
    back = lax.all_to_all(out, ("y", "core"), 0, 0, tiled=True)
    partial = _combine(z, table, back)
    return lax.psum_scatter(partial, "z", scatter_dimension=0, tiled=True)


def solution(mesh):
    fine = Mesh(mesh.devices.reshape(4, 2, 16, 4), ("x", "core", "z", "y"))
    dp, ex = ("x", "core"), ("z", "y")
    every = dp + ex
    placed = (
        P(every, None),
        P(every, None),
        P(every, None),
        P(every),
        P(ex, dp, None),
        P(ex, None, dp),
        P(ex, dp, None),
        P(ex, None, None),
    )
    return jax.shard_map(per_device, mesh=fine, in_specs=placed, out_specs=P(every, None), check_vma=False)
```

```python
import jax
import jax.numpy as jnp
from jax import lax
from jax.experimental import pallas as pl
from jax.experimental.pallas import tpu as pltpu
from jax.sharding import Mesh, PartitionSpec as P

BF = jnp.bfloat16
F16 = jnp.float16
F32 = jnp.float32
TOK = 16
TOP = 8
DEST = 16
TEN = 4
RANK = 16
PIECE = 1024
WIDE = 4096
META = 128
ROUTE_AT = 64
GATE_AT = 72
ROWS = 256
TOKS = 128
SCALE_AT = 96
LIFT = 4096.0
def _params(mib):
    return pltpu.CompilerParams(vmem_limit_bytes=mib << 20)


def _matches(meta, z1):
    lane = lax.broadcasted_iota(jnp.int32, (TOKS, META), 1)
    expert = (z1 * 2 + lane % 2) * 8 + (lane // 4) * 2 + (lane // 2) % 2
    expert = jnp.where(lane < DEST, expert, -1).astype(F32)
    return [meta[:, ROUTE_AT + k : ROUTE_AT + k + 1] == expert for k in range(TOP)]


def _spread():
    e = lax.broadcasted_iota(jnp.int32, (META, ROWS), 0)
    j = lax.broadcasted_iota(jnp.int32, (META, ROWS), 1)
    return (e == j // 16).astype(BF)


def _slots(matches):
    named = sum(m.astype(F32) for m in matches)
    row = lax.broadcasted_iota(jnp.int32, (TOKS, TOKS), 0)
    col = lax.broadcasted_iota(jnp.int32, (TOKS, TOKS), 1)
    before = ((row // TOK == col // TOK) & (col < row)).astype(BF)
    rank = jnp.dot(before, named.astype(BF), preferred_element_type=F32)
    seat = named * (rank + 1.0)
    at = jnp.dot(seat.astype(BF), _spread(), preferred_element_type=F32)
    tok = lax.broadcasted_iota(jnp.int32, (TOKS, ROWS), 0)
    slot = lax.broadcasted_iota(jnp.int32, (TOKS, ROWS), 1)
    return (at == (slot % 2 + 1).astype(F32)) & (tok // TOK == (slot % 16) // 2)


def _select_kernel(z_ref, m_ref, t_ref, o_ref):
    slots = _slots(_matches(m_ref[...].reshape(TOKS, META).astype(F32), z_ref[0])).astype(BF)
    t = t_ref[...].reshape(TOKS, t_ref.shape[2])
    out = lax.dot_general(slots, t, (((0,), (0,)), ((), ())), preferred_element_type=F32)
    o_ref[...] = out.astype(BF).reshape(o_ref.shape)


def _select(z1, table):
    width = (WIDE + META) // 3
    return pl.pallas_call(
        _select_kernel,
        grid_spec=pltpu.PrefetchScalarGridSpec(
            num_scalar_prefetch=1,
            grid=(3,),
            in_specs=[
                pl.BlockSpec((8, TOK, META), lambda g, z: (0, 0, WIDE // META)),
                pl.BlockSpec((8, TOK, width), lambda g, z: (0, 0, g)),
            ],
            out_specs=pl.BlockSpec((DEST, 16, width), lambda g, z: (0, 0, g)),
        ),
        out_shape=jax.ShapeDtypeStruct((DEST, 16, WIDE + META), BF),
        compiler_params=_params(24),
        name="select",
    )(z1, table, table)


def _up_kernel(c_ref, x_own, x_other, m_ref, t_ref, w_own, w_other, a_own, a_other, a_out, o_ref, acc, shrink):
    g = pl.program_id(0)
    lanes = (((1,), (1,)), ((), ()))
    more = jnp.dot(x_own[...], w_own[0], preferred_element_type=F32)
    more += jnp.dot(x_other[...], w_other[0], preferred_element_type=F32)
    less = lax.dot_general(x_own[...], a_own[0], lanes, preferred_element_type=F32)
    less += lax.dot_general(x_other[...], a_other[0], lanes, preferred_element_type=F32)

    @pl.when(g == 0)
    def _():
        acc[...] = more
        shrink[...] = less

    @pl.when(g > 0)
    def _():
        acc[...] += more
        shrink[...] += less

    @pl.when(g == 3)
    def _():
        kept = shrink[...] * m_ref[:, :64].astype(F32)
        high = kept.astype(BF)
        low = (kept - high.astype(F32)).astype(BF)
        v = acc[...] + jnp.dot(high, a_out[0], preferred_element_type=F32)
        v += jnp.dot(low, a_out[0], preferred_element_type=F32)
        hidden = (v / (1.0 + jnp.exp(-v))).astype(BF).astype(F32)
        peak = jnp.max(jnp.abs(hidden), axis=1, keepdims=True)
        power = jnp.floor(jnp.log2(jnp.maximum(peak, 1e-30)))
        o_ref[:, :PIECE] = (hidden * jnp.exp2(-power)).astype(BF)
        lane = lax.broadcasted_iota(jnp.int32, (ROWS, META), 1)
        meta = jnp.concatenate([t_ref[...].reshape(TOKS, META), jnp.zeros((ROWS - TOKS, META), BF)], axis=0)
        o_ref[:, PIECE:] = jnp.where(lane == SCALE_AT, power, meta.astype(F32)).astype(BF)


def _up(c, rows, table, w_own, w_other, a_in, a_out):
    own = lambda g, c: (2 * g + c[0])
    other = lambda g, c: (2 * g + 1 - c[0])
    return pl.pallas_call(
        _up_kernel,
        grid_spec=pltpu.PrefetchScalarGridSpec(
            num_scalar_prefetch=1,
            grid=(4,),
            in_specs=[
                pl.BlockSpec((ROWS, 512), lambda g, c: (0, own(g, c))),
                pl.BlockSpec((ROWS, 512), lambda g, c: (0, other(g, c))),
                pl.BlockSpec((ROWS, META), lambda g, c: (0, WIDE // META)),
                pl.BlockSpec((8, TOK, META), lambda g, c: (0, 0, WIDE // META)),
                pl.BlockSpec((1, 512, PIECE), lambda g, c: (g, 0, 0)),
                pl.BlockSpec((1, 512, PIECE), lambda g, c: (g, 0, 0)),
                pl.BlockSpec((1, 64, 512), lambda g, c: (own(g, c), 0, 0)),
                pl.BlockSpec((1, 64, 512), lambda g, c: (other(g, c), 0, 0)),
                pl.BlockSpec((1, 64, PIECE), lambda g, c: (c[0], 0, 0)),
            ],
            out_specs=pl.BlockSpec((ROWS, PIECE + META), lambda g, c: (0, 0)),
            scratch_shapes=[pltpu.VMEM((ROWS, PIECE), F32), pltpu.VMEM((ROWS, 64), F32)],
        ),
        out_shape=jax.ShapeDtypeStruct((ROWS, PIECE + META), BF),
        compiler_params=_params(32),
        name="up",
    )(c, rows, rows, rows, table, w_own, w_other, a_in, a_in, a_out)


def _down_kernel(c_ref, h_ref, m_ref, w_own, w_other, o_ref):
    scale = jnp.exp2(m_ref[0, :, SCALE_AT : SCALE_AT + 1].astype(F32))
    for side, w in ((c_ref[0], w_own[0]), (1 - c_ref[0], w_other[...])):
        cols = pl.ds(pl.multiple_of(side * 512, 512), 512)
        out = jnp.dot(h_ref[0], w, preferred_element_type=F32) * scale
        o_ref[:, :, :, cols] = out.astype(BF).reshape(DEST, 1, 16, 512)


def _down(c, hidden, w, w_other):
    return pl.pallas_call(
        _down_kernel,
        grid_spec=pltpu.PrefetchScalarGridSpec(
            num_scalar_prefetch=1,
            grid=(4,),
            in_specs=[
                pl.BlockSpec((1, ROWS, PIECE), lambda g, c: (g, 0, 0)),
                pl.BlockSpec((1, ROWS, META), lambda g, c: (g, 0, PIECE // META)),
                pl.BlockSpec((1, PIECE, 512), lambda g, c: (c[0], 0, 0)),
                pl.BlockSpec((PIECE, 512), lambda g, c: (0, 0)),
            ],
            out_specs=pl.BlockSpec((DEST, 1, 16, PIECE), lambda g, c: (0, g, 0, 0)),
        ),
        out_shape=jax.ShapeDtypeStruct((DEST, 4, 16, PIECE), BF),
        compiler_params=_params(24),
        name="down",
    )(c, hidden, hidden, w, w_other)


def _combine_kernel(z_ref, m_ref, y_ref, o_ref):
    meta = m_ref[0].astype(F32)
    matches = _matches(meta, z_ref[0])
    gate = sum(jnp.where(m, meta[:, GATE_AT + k : GATE_AT + k + 1], 0.0) for k, m in enumerate(matches))
    gates = jnp.dot(gate.astype(BF), _spread(), preferred_element_type=F32)
    weight = jnp.where(_slots(matches), gates, 0.0).astype(BF)
    out = jnp.dot(weight, y_ref[...].reshape(ROWS, PIECE), preferred_element_type=F32)
    o_ref[...] = out.astype(BF).reshape(8, 1, TOK, PIECE)


def _combine(z1, hidden, back):
    return pl.pallas_call(
        _combine_kernel,
        grid_spec=pltpu.PrefetchScalarGridSpec(
            num_scalar_prefetch=1,
            grid=(4,),
            in_specs=[
                pl.BlockSpec((1, TOKS, META), lambda g, z: (g, 0, PIECE // META)),
                pl.BlockSpec((DEST, 1, 16, PIECE), lambda g, z: (0, g, 0, 0)),
            ],
            out_specs=pl.BlockSpec((8, 1, TOK, PIECE), lambda g, z: (0, g, 0, 0)),
        ),
        out_shape=jax.ShapeDtypeStruct((8, 4, TOK, PIECE), BF),
        compiler_params=_params(24),
        name="combine",
    )(z1, hidden, back)


def _swap(v):
    return lax.ppermute(v, "core", [(0, 1), (1, 0)])


def per_device(tokens, route_ids, gate_weights, tenant_ids, up_weight, down_weight, adapter_in, adapter_out):
    z1 = lax.axis_index("z1").astype(jnp.int32).reshape(1)
    core = lax.axis_index("core").astype(jnp.int32)
    c = core.reshape(1)
    one = lambda w, i: lax.dynamic_index_in_dim(w, i, 0, keepdims=False)

    w_other = _swap(lax.all_gather(one(up_weight, 1 - core), "x", axis=0))
    w_own = lax.all_gather(one(up_weight, core), "x", axis=0)
    down_other = _swap(one(down_weight, 1 - core))

    owner = jnp.arange(TEN * RANK, dtype=jnp.int32) // RANK
    mask = (owner[None, :] == tenant_ids[:, None]).astype(F16)
    meta = jnp.concatenate(
        [mask, route_ids.astype(F16), gate_weights.astype(F16), jnp.zeros((TOK, META - 80), F16)], axis=1
    )
    mine = jnp.concatenate([(tokens.astype(F32) * LIFT).astype(F16), meta], axis=1)
    table = lax.all_gather(mine, "z1", axis=0).astype(F32)
    lift = jnp.where(jnp.arange(WIDE + META) < WIDE, 1.0 / LIFT, 1.0)
    table = (table * lift).astype(BF)
    sending = _select(z1, table)
    arrived = lax.all_to_all(sending, ("y", "core", "z0"), 0, 0, tiled=True).reshape(ROWS, WIDE + META)

    a_in = (adapter_in.transpose(0, 2, 1).astype(F32) * LIFT).astype(F16)
    a_in = lax.all_gather(a_in, ("x", "core"), axis=0)
    a_in = (lax.dynamic_index_in_dim(a_in, core, 1, keepdims=False).astype(F32) / LIFT).astype(BF)

    hidden = _up(c, arrived, table, w_own, w_other, a_in, adapter_out)
    hidden = lax.all_gather(hidden.astype(F16), "x", axis=0).astype(BF)
    out = _down(c, hidden, down_weight, down_other)
    back = lax.all_to_all(out, ("y", "core", "z0"), 0, 0, tiled=True)
    partial = _combine(z1, hidden, back)
    mixed = lax.psum_scatter(partial, "z1", scatter_dimension=0, tiled=True).reshape(4, TOK, PIECE)
    home = lax.all_to_all(mixed, "x", 0, 0, tiled=True)
    return home.transpose(1, 0, 2).reshape(TOK, WIDE)


def solution(mesh):
    fine = Mesh(mesh.devices.reshape(4, 2, 8, 2, 4), ("x", "core", "z1", "z0", "y"))
    dp, ex = ("x", "core"), ("z1", "z0", "y")
    every = dp + ex
    placed = (
        P(every, None),
        P(every, None),
        P(every, None),
        P(every),
        P(ex, dp, None),
        P(ex, None, dp),
        P(ex, dp, None),
        P(ex, None, None),
    )
    return jax.shard_map(per_device, mesh=fine, in_specs=placed, out_specs=P(every, None), check_vma=False)
```

```python
import jax
import jax.numpy as jnp
from jax import lax
from jax.experimental import pallas as pl
from jax.experimental.pallas import tpu as pltpu
from jax.sharding import Mesh, PartitionSpec as P

BF = jnp.bfloat16
F16 = jnp.float16
F32 = jnp.float32
TOK = 16
TOP = 8
DEST = 16
TEN = 4
RANK = 16
PIECE = 1024
WIDE = 4096
META = 128
ROUTE_AT = 64
GATE_AT = 72
ROWS = 256
TOKS = 128
SCALE_AT = 96
LIFT = 4096.0
def _params(mib):
    return pltpu.CompilerParams(vmem_limit_bytes=mib << 20)


def _matches(meta, z1):
    lane = lax.broadcasted_iota(jnp.int32, (TOKS, META), 1)
    expert = (z1 * 2 + lane % 2) * 8 + (lane // 4) * 2 + (lane // 2) % 2
    expert = jnp.where(lane < DEST, expert, -1).astype(F32)
    return [meta[:, ROUTE_AT + k : ROUTE_AT + k + 1] == expert for k in range(TOP)]


def _spread():
    e = lax.broadcasted_iota(jnp.int32, (META, ROWS), 0)
    j = lax.broadcasted_iota(jnp.int32, (META, ROWS), 1)
    return (e == j // 16).astype(BF)


def _slots(matches):
    named = sum(m.astype(F32) for m in matches)
    row = lax.broadcasted_iota(jnp.int32, (TOKS, TOKS), 0)
    col = lax.broadcasted_iota(jnp.int32, (TOKS, TOKS), 1)
    before = ((row // TOK == col // TOK) & (col < row)).astype(BF)
    rank = jnp.dot(before, named.astype(BF), preferred_element_type=F32)
    seat = named * (rank + 1.0)
    at = jnp.dot(seat.astype(BF), _spread(), preferred_element_type=F32)
    tok = lax.broadcasted_iota(jnp.int32, (TOKS, ROWS), 0)
    slot = lax.broadcasted_iota(jnp.int32, (TOKS, ROWS), 1)
    return (at == (slot % 2 + 1).astype(F32)) & (tok // TOK == (slot % 16) // 2)


def _select_kernel(z_ref, m_ref, t_ref, *rest):
    o_ref = rest[-1]
    slots = _slots(_matches(m_ref[...].reshape(TOKS, META).astype(F32), z_ref[0])).astype(BF)
    t = t_ref[...].reshape(TOKS, t_ref.shape[2])
    out = lax.dot_general(slots, t, (((0,), (0,)), ((), ())), preferred_element_type=F32)
    o_ref[...] = out.astype(BF).reshape(o_ref.shape)


def _select(z1, table, after):
    width = (WIDE + META) // 3
    return pl.pallas_call(
        _select_kernel,
        grid_spec=pltpu.PrefetchScalarGridSpec(
            num_scalar_prefetch=1,
            grid=(3,),
            in_specs=[
                pl.BlockSpec((8, TOK, META), lambda g, z: (0, 0, WIDE // META)),
                pl.BlockSpec((8, TOK, width), lambda g, z: (0, 0, g)),
            ]
            + [pl.BlockSpec(memory_space=pl.ANY) for _ in after],
            out_specs=pl.BlockSpec((DEST, 16, width), lambda g, z: (0, 0, g)),
        ),
        out_shape=jax.ShapeDtypeStruct((DEST, 16, WIDE + META), BF),
        compiler_params=_params(24),
        name="select",
    )(z1, table, table, *after)


def _around(g, x):
    return lax.rem(x + jnp.where(g == 0, 0, jnp.where(g == 1, 3, jnp.where(g == 2, 1, 2))), 4)


def _up_kernel(at, x_ref, m_ref, t_ref, mid, left, right, far_low, far_high, a_low, a_high, a_out, o_ref, acc, shrink):
    g = pl.program_id(0)
    lanes = (((1,), (1,)), ((), ()))

    @pl.when(g == 0)
    def _():
        acc[...] = jnp.dot(x_ref[...], mid[...], preferred_element_type=F32)
        shrink[...] = jnp.zeros_like(shrink)

    @pl.when(g == 1)
    def _():
        acc[...] += jnp.dot(x_ref[...], left[...], preferred_element_type=F32)

    @pl.when(g == 2)
    def _():
        acc[...] += jnp.dot(x_ref[...], right[...], preferred_element_type=F32)

    @pl.when(g == 3)
    def _():
        far = jnp.dot(x_ref[:, :512], far_low[...], preferred_element_type=F32)
        far += jnp.dot(x_ref[:, 512:], far_high[...], preferred_element_type=F32)
        acc[...] += far

    less = lax.dot_general(x_ref[:, :512], a_low[0], lanes, preferred_element_type=F32)
    less += lax.dot_general(x_ref[:, 512:], a_high[0], lanes, preferred_element_type=F32)
    shrink[...] += less

    @pl.when(g == 3)
    def _():
        kept = shrink[...] * m_ref[:, :64].astype(F32)
        high = kept.astype(BF)
        low = (kept - high.astype(F32)).astype(BF)
        v = acc[...] + jnp.dot(high, a_out[0], preferred_element_type=F32)
        v += jnp.dot(low, a_out[0], preferred_element_type=F32)
        hidden = (v / (1.0 + jnp.exp(-v))).astype(BF).astype(F32)
        peak = jnp.max(jnp.abs(hidden), axis=1, keepdims=True)
        power = jnp.floor(jnp.log2(jnp.maximum(peak, 1e-30)))
        o_ref[:, :PIECE] = (hidden * jnp.exp2(-power)).astype(BF)
        lane = lax.broadcasted_iota(jnp.int32, (ROWS, META), 1)
        meta = jnp.concatenate([t_ref[...].reshape(TOKS, META), jnp.zeros((ROWS - TOKS, META), BF)], axis=0)
        o_ref[:, PIECE:] = jnp.where(lane == SCALE_AT, power, meta.astype(F32)).astype(BF)


def _up(at, rows, table, w, a_in, a_out):
    return pl.pallas_call(
        _up_kernel,
        grid_spec=pltpu.PrefetchScalarGridSpec(
            num_scalar_prefetch=1,
            grid=(4,),
            in_specs=[
                pl.BlockSpec((ROWS, PIECE), lambda g, at: (0, _around(g, at[1]))),
                pl.BlockSpec((ROWS, META), lambda g, at: (0, WIDE // META)),
                pl.BlockSpec((8, TOK, META), lambda g, at: (0, 0, WIDE // META)),
            ]
            + [pl.BlockSpec(p.shape, lambda g, at: (0, 0)) for p in w]
            + [
                pl.BlockSpec((1, 64, 512), lambda g, at: (2 * _around(g, at[1]), 0, 0)),
                pl.BlockSpec((1, 64, 512), lambda g, at: (2 * _around(g, at[1]) + 1, 0, 0)),
                pl.BlockSpec((1, 64, PIECE), lambda g, at: (at[0], 0, 0)),
            ],
            out_specs=pl.BlockSpec((ROWS, PIECE + META), lambda g, at: (0, 0)),
            scratch_shapes=[pltpu.VMEM((ROWS, PIECE), F32), pltpu.VMEM((ROWS, 64), F32)],
        ),
        out_shape=jax.ShapeDtypeStruct((ROWS, PIECE + META), BF),
        compiler_params=_params(32),
        name="up",
    )(at, rows, rows, table, *w, a_in, a_in, a_out)


def _down_kernel(c_ref, h_ref, m_ref, w_own, w_other, o_ref):
    scale = jnp.exp2(m_ref[0, :, SCALE_AT : SCALE_AT + 1].astype(F32))
    for side, w in ((c_ref[0], w_own[0]), (1 - c_ref[0], w_other[...])):
        cols = pl.ds(pl.multiple_of(side * 512, 512), 512)
        out = jnp.dot(h_ref[0], w, preferred_element_type=F32) * scale
        o_ref[:, :, :, cols] = out.astype(BF).reshape(DEST, 1, 16, 512)


def _down(c, hidden, w, w_other):
    return pl.pallas_call(
        _down_kernel,
        grid_spec=pltpu.PrefetchScalarGridSpec(
            num_scalar_prefetch=1,
            grid=(4,),
            in_specs=[
                pl.BlockSpec((1, ROWS, PIECE), lambda g, c: (g, 0, 0)),
                pl.BlockSpec((1, ROWS, META), lambda g, c: (g, 0, PIECE // META)),
                pl.BlockSpec((1, PIECE, 512), lambda g, c: (c[0], 0, 0)),
                pl.BlockSpec((PIECE, 512), lambda g, c: (0, 0)),
            ],
            out_specs=pl.BlockSpec((DEST, 1, 16, PIECE), lambda g, c: (0, g, 0, 0)),
        ),
        out_shape=jax.ShapeDtypeStruct((DEST, 4, 16, PIECE), BF),
        compiler_params=_params(24),
        name="down",
    )(c, hidden, hidden, w, w_other)


def _combine_kernel(z_ref, m_ref, y_ref, o_ref):
    meta = m_ref[0].astype(F32)
    matches = _matches(meta, z_ref[0])
    gate = sum(jnp.where(m, meta[:, GATE_AT + k : GATE_AT + k + 1], 0.0) for k, m in enumerate(matches))
    gates = jnp.dot(gate.astype(BF), _spread(), preferred_element_type=F32)
    weight = jnp.where(_slots(matches), gates, 0.0).astype(BF)
    out = jnp.dot(weight, y_ref[...].reshape(ROWS, PIECE), preferred_element_type=F32)
    o_ref[...] = out.astype(BF).reshape(8, 1, TOK, PIECE)


def _combine(z1, hidden, back):
    return pl.pallas_call(
        _combine_kernel,
        grid_spec=pltpu.PrefetchScalarGridSpec(
            num_scalar_prefetch=1,
            grid=(4,),
            in_specs=[
                pl.BlockSpec((1, TOKS, META), lambda g, z: (g, 0, PIECE // META)),
                pl.BlockSpec((DEST, 1, 16, PIECE), lambda g, z: (0, g, 0, 0)),
            ],
            out_specs=pl.BlockSpec((8, 1, TOK, PIECE), lambda g, z: (0, g, 0, 0)),
        ),
        out_shape=jax.ShapeDtypeStruct((8, 4, TOK, PIECE), BF),
        compiler_params=_params(24),
        name="combine",
    )(z1, hidden, back)


def _shift_x(v, by):
    return lax.ppermute(v, "x", [(i, (i + by) % 4) for i in range(4)])


def _gather_x(w):
    k = w.shape[0] // 2
    left, right = _shift_x(w, 1), _shift_x(w, -1)
    return [w, left, right, _shift_x(left[:k], 1), _shift_x(right[k:], -1)]


def _swap(v):
    return lax.ppermute(v, "core", [(0, 1), (1, 0)])


def per_device(tokens, route_ids, gate_weights, tenant_ids, up_weight, down_weight, adapter_in, adapter_out):
    z1 = lax.axis_index("z1").astype(jnp.int32).reshape(1)
    core = lax.axis_index("core").astype(jnp.int32)
    c = core.reshape(1)
    at = jnp.stack([core, lax.axis_index("x").astype(jnp.int32)])
    one = lambda w, i: lax.dynamic_index_in_dim(w, i, 0, keepdims=False)

    up_own, up_other = one(up_weight, core), _swap(one(up_weight, 1 - core))
    first, second = jnp.where(core == 0, up_own, up_other), jnp.where(core == 0, up_other, up_own)
    w_up = _gather_x(jnp.concatenate([first, second], axis=0))
    down_other = _swap(one(down_weight, 1 - core))

    owner = jnp.arange(TEN * RANK, dtype=jnp.int32) // RANK
    mask = (owner[None, :] == tenant_ids[:, None]).astype(F16)
    meta = jnp.concatenate(
        [mask, route_ids.astype(F16), gate_weights.astype(F16), jnp.zeros((TOK, META - 80), F16)], axis=1
    )
    mine = jnp.concatenate([(tokens.astype(F32) * LIFT).astype(F16), meta], axis=1)
    table = lax.all_gather(mine, "z1", axis=0).astype(F32)
    lift = jnp.where(jnp.arange(WIDE + META) < WIDE, 1.0 / LIFT, 1.0)
    table = (table * lift).astype(BF)
    sending = _select(z1, table, w_up[1:3])
    arrived = lax.all_to_all(sending, ("y", "core", "z0"), 0, 0, tiled=True).reshape(ROWS, WIDE + META)

    a_in = (adapter_in.transpose(0, 2, 1).astype(F32) * LIFT).astype(F16)
    a_in = lax.all_gather(a_in, ("x", "core"), axis=0)
    a_in = (lax.dynamic_index_in_dim(a_in, core, 1, keepdims=False).astype(F32) / LIFT).astype(BF)

    hidden = _up(at, arrived, table, w_up, a_in, adapter_out)
    hidden = lax.all_gather(hidden.astype(F16), "x", axis=0).astype(BF)
    out = _down(c, hidden, down_weight, down_other)
    back = lax.all_to_all(out, ("y", "core", "z0"), 0, 0, tiled=True)
    partial = _combine(z1, hidden, back)
    mixed = lax.psum_scatter(partial, "z1", scatter_dimension=0, tiled=True).reshape(4, TOK, PIECE)
    home = lax.all_to_all(mixed, "x", 0, 0, tiled=True)
    return home.transpose(1, 0, 2).reshape(TOK, WIDE)


def solution(mesh):
    fine = Mesh(mesh.devices.reshape(4, 2, 8, 2, 4), ("x", "core", "z1", "z0", "y"))
    dp, ex = ("x", "core"), ("z1", "z0", "y")
    every = dp + ex
    placed = (
        P(every, None),
        P(every, None),
        P(every, None),
        P(every),
        P(ex, dp, None),
        P(ex, None, dp),
        P(ex, dp, None),
        P(ex, None, None),
    )
    return jax.shard_map(per_device, mesh=fine, in_specs=placed, out_specs=P(every, None), check_vma=False)
```

```python
import jax
import jax.numpy as jnp
from jax import lax
from jax.experimental import pallas as pl
from jax.experimental.pallas import tpu as pltpu
from jax.sharding import Mesh, PartitionSpec as P

BF = jnp.bfloat16
F16 = jnp.float16
F32 = jnp.float32
TOK = 16
TOP = 8
DEST = 16
TEN = 4
RANK = 16
PIECE = 1024
WIDE = 4096
META = 128
ROUTE_AT = 64
GATE_AT = 72
ROWS = 256
TOKS = 128
LIFT = 4096.0
def _params(mib):
    return pltpu.CompilerParams(vmem_limit_bytes=mib << 20)


def _matches(meta, z1):
    lane = lax.broadcasted_iota(jnp.int32, (TOKS, META), 1)
    expert = (z1 * 2 + lane % 2) * 8 + (lane // 4) * 2 + (lane // 2) % 2
    expert = jnp.where(lane < DEST, expert, -1).astype(F32)
    return [meta[:, ROUTE_AT + k : ROUTE_AT + k + 1] == expert for k in range(TOP)]


def _spread():
    e = lax.broadcasted_iota(jnp.int32, (META, ROWS), 0)
    j = lax.broadcasted_iota(jnp.int32, (META, ROWS), 1)
    return (e == j // 16).astype(BF)


def _slots(matches):
    named = sum(m.astype(F32) for m in matches)
    row = lax.broadcasted_iota(jnp.int32, (TOKS, TOKS), 0)
    col = lax.broadcasted_iota(jnp.int32, (TOKS, TOKS), 1)
    before = ((row // TOK == col // TOK) & (col < row)).astype(BF)
    rank = jnp.dot(before, named.astype(BF), preferred_element_type=F32)
    seat = named * (rank + 1.0)
    at = jnp.dot(seat.astype(BF), _spread(), preferred_element_type=F32)
    tok = lax.broadcasted_iota(jnp.int32, (TOKS, ROWS), 0)
    slot = lax.broadcasted_iota(jnp.int32, (TOKS, ROWS), 1)
    return (at == (slot % 2 + 1).astype(F32)) & (tok // TOK == (slot % 16) // 2)


def _select_kernel(z_ref, m_ref, t_ref, *rest):
    o_ref = rest[-1]
    slots = _slots(_matches(m_ref[...].reshape(TOKS, META).astype(F32), z_ref[0])).astype(BF)
    t = t_ref[...].reshape(TOKS, t_ref.shape[2])
    out = lax.dot_general(slots, t, (((0,), (0,)), ((), ())), preferred_element_type=F32)
    o_ref[...] = out.astype(BF).reshape(o_ref.shape)


def _select(z1, table, after):
    width = (WIDE + META) // 3
    return pl.pallas_call(
        _select_kernel,
        grid_spec=pltpu.PrefetchScalarGridSpec(
            num_scalar_prefetch=1,
            grid=(3,),
            in_specs=[
                pl.BlockSpec((8, TOK, META), lambda g, z: (0, 0, WIDE // META)),
                pl.BlockSpec((8, TOK, width), lambda g, z: (0, 0, g)),
            ]
            + [pl.BlockSpec(memory_space=pl.ANY) for _ in after],
            out_specs=pl.BlockSpec((DEST, 16, width), lambda g, z: (0, 0, g)),
        ),
        out_shape=jax.ShapeDtypeStruct((DEST, 16, WIDE + META), BF),
        compiler_params=_params(24),
        name="select",
    )(z1, table, table, *after)


def _around(g, x):
    return lax.rem(x + jnp.where(g == 0, 0, jnp.where(g == 1, 3, jnp.where(g == 2, 1, 2))), 4)


def _up_kernel(at, x_ref, m_ref, mid, left, right, far_low, far_high, a_low, a_high, a_out, o_ref, acc, shrink):
    g = pl.program_id(0)
    lanes = (((1,), (1,)), ((), ()))

    @pl.when(g == 0)
    def _():
        acc[...] = jnp.dot(x_ref[...], mid[...], preferred_element_type=F32)
        shrink[...] = jnp.zeros_like(shrink)

    @pl.when(g == 1)
    def _():
        acc[...] += jnp.dot(x_ref[...], left[...], preferred_element_type=F32)

    @pl.when(g == 2)
    def _():
        acc[...] += jnp.dot(x_ref[...], right[...], preferred_element_type=F32)

    @pl.when(g == 3)
    def _():
        far = jnp.dot(x_ref[:, :512], far_low[...], preferred_element_type=F32)
        far += jnp.dot(x_ref[:, 512:], far_high[...], preferred_element_type=F32)
        acc[...] += far

    less = lax.dot_general(x_ref[:, :512], a_low[0, 0], lanes, preferred_element_type=F32)
    less += lax.dot_general(x_ref[:, 512:], a_high[0, 0], lanes, preferred_element_type=F32)
    shrink[...] += less

    @pl.when(g == 3)
    def _():
        kept = shrink[...] * m_ref[:, :64].astype(F32)
        high = kept.astype(BF)
        low = (kept - high.astype(F32)).astype(BF)
        v = acc[...] + jnp.dot(high, a_out[0], preferred_element_type=F32)
        v += jnp.dot(low, a_out[0], preferred_element_type=F32)
        hidden = (v / (1.0 + jnp.exp(-v))).astype(BF).astype(F32)
        peak = jnp.max(jnp.abs(hidden), axis=1, keepdims=True)
        power = jnp.floor(jnp.log2(jnp.maximum(peak, 1e-30)))
        o_ref[:, :PIECE] = (hidden * jnp.exp2(-power)).astype(BF)
        o_ref[:, PIECE:] = jnp.broadcast_to(power, (ROWS, META)).astype(BF)


def _up(at, rows, w, a_in, a_out):
    return pl.pallas_call(
        _up_kernel,
        grid_spec=pltpu.PrefetchScalarGridSpec(
            num_scalar_prefetch=1,
            grid=(4,),
            in_specs=[
                pl.BlockSpec((ROWS, PIECE), lambda g, at: (0, _around(g, at[1]))),
                pl.BlockSpec((ROWS, META), lambda g, at: (0, WIDE // META)),
            ]
            + [pl.BlockSpec(p.shape, lambda g, at: (0, 0)) for p in w]
            + [
                pl.BlockSpec((1, 1, 64, 512), lambda g, at: (2 * _around(g, at[1]), at[0], 0, 0)),
                pl.BlockSpec((1, 1, 64, 512), lambda g, at: (2 * _around(g, at[1]) + 1, at[0], 0, 0)),
                pl.BlockSpec((1, 64, PIECE), lambda g, at: (at[0], 0, 0)),
            ],
            out_specs=pl.BlockSpec((ROWS, PIECE + META), lambda g, at: (0, 0)),
            scratch_shapes=[pltpu.VMEM((ROWS, PIECE), F32), pltpu.VMEM((ROWS, 64), F32)],
        ),
        out_shape=jax.ShapeDtypeStruct((ROWS, PIECE + META), BF),
        compiler_params=_params(32),
        name="up",
    )(at, rows, rows, *w, a_in, a_in, a_out)


def _down_kernel(c_ref, h_ref, m_ref, w_own, w_other, o_ref):
    scale = jnp.exp2(m_ref[0, :, :1].astype(F32))
    for side, w in ((c_ref[0], w_own[0]), (1 - c_ref[0], w_other[...])):
        cols = pl.ds(pl.multiple_of(side * 512, 512), 512)
        out = jnp.dot(h_ref[0], w, preferred_element_type=F32) * scale
        o_ref[:, :, :, cols] = out.astype(BF).reshape(1, DEST, 16, 512)


def _down(c, hidden, w, w_other):
    return pl.pallas_call(
        _down_kernel,
        grid_spec=pltpu.PrefetchScalarGridSpec(
            num_scalar_prefetch=1,
            grid=(4,),
            in_specs=[
                pl.BlockSpec((1, ROWS, PIECE), lambda g, c: (g, 0, 0)),
                pl.BlockSpec((1, ROWS, META), lambda g, c: (g, 0, PIECE // META)),
                pl.BlockSpec((1, PIECE, 512), lambda g, c: (c[0], 0, 0)),
                pl.BlockSpec((PIECE, 512), lambda g, c: (0, 0)),
            ],
            out_specs=pl.BlockSpec((1, DEST, 16, PIECE), lambda g, c: (g, 0, 0, 0)),
        ),
        out_shape=jax.ShapeDtypeStruct((4, DEST, 16, PIECE), BF),
        compiler_params=_params(24),
        name="down",
    )(c, hidden, hidden, w, w_other)


def _combine_kernel(z_ref, m_ref, y_ref, o_ref, weight):
    @pl.when(pl.program_id(0) == 0)
    def _():
        meta = m_ref[...].reshape(TOKS, META).astype(F32)
        matches = _matches(meta, z_ref[0])
        gate = sum(jnp.where(m, meta[:, GATE_AT + k : GATE_AT + k + 1], 0.0) for k, m in enumerate(matches))
        gates = jnp.dot(gate.astype(BF), _spread(), preferred_element_type=F32)
        weight[...] = jnp.where(_slots(matches), gates, 0.0).astype(BF)

    out = jnp.dot(weight[...], y_ref[...].reshape(ROWS, PIECE), preferred_element_type=F32)
    o_ref[...] = out.astype(BF)


def _combine(z1, table, back):
    return pl.pallas_call(
        _combine_kernel,
        grid_spec=pltpu.PrefetchScalarGridSpec(
            num_scalar_prefetch=1,
            grid=(4,),
            in_specs=[
                pl.BlockSpec((8, TOK, META), lambda g, z: (0, 0, WIDE // META)),
                pl.BlockSpec((1, DEST, 16, PIECE), lambda g, z: (g, 0, 0, 0)),
            ],
            out_specs=pl.BlockSpec((TOKS, PIECE), lambda g, z: (0, g)),
            scratch_shapes=[pltpu.VMEM((TOKS, ROWS), BF)],
        ),
        out_shape=jax.ShapeDtypeStruct((TOKS, WIDE), BF),
        compiler_params=_params(24),
        name="combine",
    )(z1, table, back)


def _shift_x(v, by):
    return lax.ppermute(v, "x", [(i, (i + by) % 4) for i in range(4)])


def _gather_x(w):
    k = w.shape[0] // 2
    left, right = _shift_x(w, 1), _shift_x(w, -1)
    return [w, left, right, _shift_x(left[:k], 1), _shift_x(right[k:], -1)]


def _swap(v):
    return lax.ppermute(v, "core", [(0, 1), (1, 0)])


def per_device(tokens, route_ids, gate_weights, tenant_ids, up_weight, down_weight, adapter_in, adapter_out):
    z1 = lax.axis_index("z1").astype(jnp.int32).reshape(1)
    core = lax.axis_index("core").astype(jnp.int32)
    c = core.reshape(1)
    at = jnp.stack([core, lax.axis_index("x").astype(jnp.int32)])
    one = lambda w, i: lax.dynamic_index_in_dim(w, i, 0, keepdims=False)

    up_own, up_other = one(up_weight, core), _swap(one(up_weight, 1 - core))
    first, second = jnp.where(core == 0, up_own, up_other), jnp.where(core == 0, up_other, up_own)
    w_up = _gather_x(jnp.concatenate([first, second], axis=0))
    a_in = lax.all_gather(adapter_in.transpose(0, 2, 1), ("x", "core"), axis=0)
    down_other = _swap(one(down_weight, 1 - core))

    owner = jnp.arange(TEN * RANK, dtype=jnp.int32) // RANK
    mask = (owner[None, :] == tenant_ids[:, None]).astype(F16)
    meta = jnp.concatenate(
        [mask, route_ids.astype(F16), gate_weights.astype(F16), jnp.zeros((TOK, META - 80), F16)], axis=1
    )
    mine = jnp.concatenate([(tokens.astype(F32) * LIFT).astype(F16), meta], axis=1)
    table = lax.all_gather(mine, "z1", axis=0).astype(F32)
    lift = jnp.where(jnp.arange(WIDE + META) < WIDE, 1.0 / LIFT, 1.0)
    table = (table * lift).astype(BF)
    sending = _select(z1, table, w_up[1:3] + [a_in])
    arrived = lax.all_to_all(sending, ("y", "core", "z0"), 0, 0, tiled=True).reshape(ROWS, WIDE + META)

    hidden = _up(at, arrived, w_up, a_in, adapter_out)
    hidden = lax.all_gather(hidden.astype(F16), "x", axis=0).astype(BF)
    out = _down(c, hidden, down_weight, down_other)
    back = lax.all_to_all(out.reshape(64, 16, PIECE), ("x", "y", "core", "z0"), 0, 0, tiled=True)
    partial = _combine(z1, table, back.reshape(4, DEST, 16, PIECE))
    return lax.psum_scatter(partial, "z1", scatter_dimension=0, tiled=True)


def solution(mesh):
    fine = Mesh(mesh.devices.reshape(4, 2, 8, 2, 4), ("x", "core", "z1", "z0", "y"))
    dp, ex = ("x", "core"), ("z1", "z0", "y")
    every = dp + ex
    placed = (
        P(every, None),
        P(every, None),
        P(every, None),
        P(every),
        P(ex, dp, None),
        P(ex, None, dp),
        P(ex, dp, None),
        P(ex, None, None),
    )
    return jax.shard_map(per_device, mesh=fine, in_specs=placed, out_specs=P(every, None), check_vma=False)
```

```python
import jax
import jax.numpy as jnp
from jax import lax
from jax.experimental import pallas as pl
from jax.experimental.pallas import tpu as pltpu
from jax.sharding import Mesh, PartitionSpec as P

BF = jnp.bfloat16
F16 = jnp.float16
F32 = jnp.float32
TOK = 16
TOP = 8
DEST = 16
TEN = 4
RANK = 16
PIECE = 1024
WIDE = 4096
META = 128
ROUTE_AT = 64
GATE_AT = 72
ROWS = 256
TOKS = 128
LIFT = 4096.0
def _params(mib):
    return pltpu.CompilerParams(vmem_limit_bytes=mib << 20)


def _matches(meta, z1):
    lane = lax.broadcasted_iota(jnp.int32, (TOKS, META), 1)
    expert = (z1 * 2 + lane % 2) * 8 + (lane // 4) * 2 + (lane // 2) % 2
    expert = jnp.where(lane < DEST, expert, -1).astype(F32)
    return [meta[:, ROUTE_AT + k : ROUTE_AT + k + 1] == expert for k in range(TOP)]


def _spread():
    e = lax.broadcasted_iota(jnp.int32, (META, ROWS), 0)
    j = lax.broadcasted_iota(jnp.int32, (META, ROWS), 1)
    return (e == j // 16).astype(BF)


def _slots(matches):
    named = sum(m.astype(F32) for m in matches)
    row = lax.broadcasted_iota(jnp.int32, (TOKS, TOKS), 0)
    col = lax.broadcasted_iota(jnp.int32, (TOKS, TOKS), 1)
    before = ((row // TOK == col // TOK) & (col < row)).astype(BF)
    rank = jnp.dot(before, named.astype(BF), preferred_element_type=F32)
    seat = named * (rank + 1.0)
    at = jnp.dot(seat.astype(BF), _spread(), preferred_element_type=F32)
    tok = lax.broadcasted_iota(jnp.int32, (TOKS, ROWS), 0)
    slot = lax.broadcasted_iota(jnp.int32, (TOKS, ROWS), 1)
    return (at == (slot % 2 + 1).astype(F32)) & (tok // TOK == (slot % 16) // 2)


def _select_kernel(z_ref, m_ref, t_ref, *rest):
    o_ref = rest[-1]
    slots = _slots(_matches(m_ref[...].reshape(TOKS, META).astype(F32), z_ref[0])).astype(BF)
    t = t_ref[...].reshape(TOKS, t_ref.shape[2])
    out = lax.dot_general(slots, t, (((0,), (0,)), ((), ())), preferred_element_type=F32)
    o_ref[...] = out.astype(BF).reshape(o_ref.shape)


def _select(z1, table, after):
    width = (WIDE + META) // 3
    return pl.pallas_call(
        _select_kernel,
        grid_spec=pltpu.PrefetchScalarGridSpec(
            num_scalar_prefetch=1,
            grid=(3,),
            in_specs=[
                pl.BlockSpec((8, TOK, META), lambda g, z: (0, 0, WIDE // META)),
                pl.BlockSpec((8, TOK, width), lambda g, z: (0, 0, g)),
            ]
            + [pl.BlockSpec(memory_space=pl.ANY) for _ in after],
            out_specs=pl.BlockSpec((DEST, 16, width), lambda g, z: (0, 0, g)),
        ),
        out_shape=jax.ShapeDtypeStruct((DEST, 16, WIDE + META), BF),
        compiler_params=_params(24),
        name="select",
    )(z1, table, table, *after)


HELD = ((0, 0, 768), (0, 768, 256), (3, 0, 768), (3, 768, 256), (1, 256, 768), (1, 0, 256), (2, 0, 512), (2, 512, 512))


def _up_kernel(at, x_ref, *refs):
    w = refs[: len(HELD)]
    a_in, a_out, o_ref, high, low, hidden = refs[len(HELD) :]
    g = pl.program_id(0)

    @pl.when(g == 0)
    def _():
        kept = jnp.zeros((ROWS, 64), F32)
        for i in range(8):
            part = x_ref[:, i * 512 : i * 512 + 512]
            kept += lax.dot_general(part, a_in[i, 0], (((1,), (1,)), ((), ())), preferred_element_type=F32)
        kept *= x_ref[:, WIDE : WIDE + 64].astype(F32)
        high[...] = kept.astype(BF)
        low[...] = (kept - high[...].astype(F32)).astype(BF)

    v = jnp.dot(high[...], a_out[0], preferred_element_type=F32)
    v += jnp.dot(low[...], a_out[0], preferred_element_type=F32)
    for ref, (away, start, size) in zip(w, HELD):
        first = pl.multiple_of(lax.rem(at[1] + away, 4) * PIECE + start, 256)
        v += jnp.dot(x_ref[:, pl.ds(first, size)], ref[...], preferred_element_type=F32)
    hidden[g] = (v / (1.0 + jnp.exp(-v))).astype(BF).astype(F32)

    @pl.when(g == 3)
    def _():
        peak = jnp.max(jnp.abs(hidden[0]), axis=1, keepdims=True)
        for i in range(1, 4):
            peak = jnp.maximum(peak, jnp.max(jnp.abs(hidden[i]), axis=1, keepdims=True))
        power = jnp.floor(jnp.log2(jnp.maximum(peak, 1e-30)))
        scale = jnp.exp2(-power)
        for i in range(4):
            o_ref[:, i * 256 : i * 256 + 256] = (hidden[i] * scale).astype(BF)
        o_ref[:, PIECE:] = jnp.broadcast_to(power, (ROWS, META)).astype(BF)


def _up(at, rows, w, a_in, a_out):
    return pl.pallas_call(
        _up_kernel,
        grid_spec=pltpu.PrefetchScalarGridSpec(
            num_scalar_prefetch=1,
            grid=(4,),
            in_specs=[pl.BlockSpec((ROWS, WIDE + META), lambda g, at: (0, 0))]
            + [pl.BlockSpec((p.shape[0], 256), lambda g, at: (0, g)) for p in w]
            + [
                pl.BlockSpec((8, 1, 64, 512), lambda g, at: (0, at[0], 0, 0)),
                pl.BlockSpec((1, 64, 256), lambda g, at: (at[0], 0, g)),
            ],
            out_specs=pl.BlockSpec((ROWS, PIECE + META), lambda g, at: (0, 0)),
            scratch_shapes=[
                pltpu.VMEM((ROWS, 64), BF),
                pltpu.VMEM((ROWS, 64), BF),
                pltpu.VMEM((4, ROWS, 256), F32),
            ],
        ),
        out_shape=jax.ShapeDtypeStruct((ROWS, PIECE + META), BF),
        compiler_params=_params(32),
        name="up",
    )(at, rows, *w, a_in, a_out)


def _down_kernel(c_ref, h_ref, m_ref, w_own, w_other, o_ref):
    scale = jnp.exp2(m_ref[0, :, :1].astype(F32))
    for side, w in ((c_ref[0], w_own[0]), (1 - c_ref[0], w_other[...])):
        cols = pl.ds(pl.multiple_of(side * 512, 512), 512)
        out = jnp.dot(h_ref[0], w, preferred_element_type=F32) * scale
        o_ref[:, :, :, cols] = out.astype(BF).reshape(1, DEST, 16, 512)


def _down(c, hidden, w, w_other):
    return pl.pallas_call(
        _down_kernel,
        grid_spec=pltpu.PrefetchScalarGridSpec(
            num_scalar_prefetch=1,
            grid=(4,),
            in_specs=[
                pl.BlockSpec((1, ROWS, PIECE), lambda g, c: (g, 0, 0)),
                pl.BlockSpec((1, ROWS, META), lambda g, c: (g, 0, PIECE // META)),
                pl.BlockSpec((1, PIECE, 512), lambda g, c: (c[0], 0, 0)),
                pl.BlockSpec((PIECE, 512), lambda g, c: (0, 0)),
            ],
            out_specs=pl.BlockSpec((1, DEST, 16, PIECE), lambda g, c: (g, 0, 0, 0)),
        ),
        out_shape=jax.ShapeDtypeStruct((4, DEST, 16, PIECE), BF),
        compiler_params=_params(24),
        name="down",
    )(c, hidden, hidden, w, w_other)


def _combine_kernel(z_ref, m_ref, y_ref, o_ref, weight):
    @pl.when(pl.program_id(0) == 0)
    def _():
        meta = m_ref[...].reshape(TOKS, META).astype(F32)
        matches = _matches(meta, z_ref[0])
        gate = sum(jnp.where(m, meta[:, GATE_AT + k : GATE_AT + k + 1], 0.0) for k, m in enumerate(matches))
        gates = jnp.dot(gate.astype(BF), _spread(), preferred_element_type=F32)
        weight[...] = jnp.where(_slots(matches), gates, 0.0).astype(BF)

    out = jnp.dot(weight[...], y_ref[...].reshape(ROWS, PIECE), preferred_element_type=F32)
    o_ref[...] = out.astype(BF)


def _combine(z1, table, back):
    return pl.pallas_call(
        _combine_kernel,
        grid_spec=pltpu.PrefetchScalarGridSpec(
            num_scalar_prefetch=1,
            grid=(4,),
            in_specs=[
                pl.BlockSpec((8, TOK, META), lambda g, z: (0, 0, WIDE // META)),
                pl.BlockSpec((1, DEST, 16, PIECE), lambda g, z: (g, 0, 0, 0)),
            ],
            out_specs=pl.BlockSpec((TOKS, PIECE), lambda g, z: (0, g)),
            scratch_shapes=[pltpu.VMEM((TOKS, ROWS), BF)],
        ),
        out_shape=jax.ShapeDtypeStruct((TOKS, WIDE), BF),
        compiler_params=_params(24),
        name="combine",
    )(z1, table, back)


def _shift_x(v, by):
    return lax.ppermute(v, "x", [(i, (i + by) % 4) for i in range(4)])


def _gather_x(first, second):
    wide, tail = jnp.concatenate([first, second[:256]], axis=0), second[256:]
    broad, head = jnp.concatenate([first[256:], second], axis=0), first[:256]
    left, right = _shift_x(wide, 1), _shift_x(broad, -1)
    far = [_shift_x(left[:512], 1), _shift_x(right[256:], -1)]
    return [wide, tail, left, _shift_x(tail, 1), right, _shift_x(head, -1)] + far


def _swap(v):
    return lax.ppermute(v, "core", [(0, 1), (1, 0)])


def per_device(tokens, route_ids, gate_weights, tenant_ids, up_weight, down_weight, adapter_in, adapter_out):
    z1 = lax.axis_index("z1").astype(jnp.int32).reshape(1)
    core = lax.axis_index("core").astype(jnp.int32)
    c = core.reshape(1)
    at = jnp.stack([core, lax.axis_index("x").astype(jnp.int32)])
    one = lambda w, i: lax.dynamic_index_in_dim(w, i, 0, keepdims=False)

    up_own, up_other = one(up_weight, core), _swap(one(up_weight, 1 - core))
    first, second = jnp.where(core == 0, up_own, up_other), jnp.where(core == 0, up_other, up_own)
    w_up = _gather_x(first, second)
    a_in = lax.all_gather(adapter_in.transpose(0, 2, 1), ("x", "core"), axis=0)
    down_other = _swap(one(down_weight, 1 - core))

    owner = jnp.arange(TEN * RANK, dtype=jnp.int32) // RANK
    mask = (owner[None, :] == tenant_ids[:, None]).astype(F16)
    meta = jnp.concatenate(
        [mask, route_ids.astype(F16), gate_weights.astype(F16), jnp.zeros((TOK, META - 80), F16)], axis=1
    )
    mine = jnp.concatenate([(tokens.astype(F32) * LIFT).astype(F16), meta], axis=1)
    table = lax.all_gather(mine, "z1", axis=0).astype(F32)
    lift = jnp.where(jnp.arange(WIDE + META) < WIDE, 1.0 / LIFT, 1.0)
    table = (table * lift).astype(BF)
    sending = _select(z1, table, [w_up[2], w_up[4], a_in])
    arrived = lax.all_to_all(sending, ("y", "core", "z0"), 0, 0, tiled=True).reshape(ROWS, WIDE + META)

    hidden = _up(at, arrived, w_up, a_in, adapter_out)
    hidden = lax.all_gather(hidden.astype(F16), "x", axis=0).astype(BF)
    out = _down(c, hidden, down_weight, down_other)
    back = lax.all_to_all(out.reshape(64, 16, PIECE), ("x", "y", "core", "z0"), 0, 0, tiled=True)
    partial = _combine(z1, table, back.reshape(4, DEST, 16, PIECE))
    return lax.psum_scatter(partial, "z1", scatter_dimension=0, tiled=True)


def solution(mesh):
    fine = Mesh(mesh.devices.reshape(4, 2, 8, 2, 4), ("x", "core", "z1", "z0", "y"))
    dp, ex = ("x", "core"), ("z1", "z0", "y")
    every = dp + ex
    placed = (
        P(every, None),
        P(every, None),
        P(every, None),
        P(every),
        P(ex, dp, None),
        P(ex, None, dp),
        P(ex, dp, None),
        P(ex, None, None),
    )
    return jax.shard_map(per_device, mesh=fine, in_specs=placed, out_specs=P(every, None), check_vma=False)
```

```python
import jax
import jax.numpy as jnp
from jax import lax
from jax.experimental import pallas as pl
from jax.experimental.pallas import tpu as pltpu
from jax.sharding import Mesh, PartitionSpec as P

BF = jnp.bfloat16
F16 = jnp.float16
F32 = jnp.float32
TOK = 16
TOP = 8
DEST = 16
TEN = 4
RANK = 16
PIECE = 1024
WIDE = 4096
META = 128
ROUTE_AT = 64
GATE_AT = 72
ROWS = 256
TOKS = 128
LIFT = 4096.0
def _params(mib):
    return pltpu.CompilerParams(vmem_limit_bytes=mib << 20)


def _matches(meta, z1):
    lane = lax.broadcasted_iota(jnp.int32, (TOKS, META), 1)
    expert = (z1 * 2 + lane % 2) * 8 + (lane // 4) * 2 + (lane // 2) % 2
    expert = jnp.where(lane < DEST, expert, -1).astype(F32)
    return [meta[:, ROUTE_AT + k : ROUTE_AT + k + 1] == expert for k in range(TOP)]


def _spread():
    e = lax.broadcasted_iota(jnp.int32, (META, ROWS), 0)
    j = lax.broadcasted_iota(jnp.int32, (META, ROWS), 1)
    return (e == j // 16).astype(BF)


def _slots(matches):
    named = sum(m.astype(F32) for m in matches)
    row = lax.broadcasted_iota(jnp.int32, (TOKS, TOKS), 0)
    col = lax.broadcasted_iota(jnp.int32, (TOKS, TOKS), 1)
    before = ((row // TOK == col // TOK) & (col < row)).astype(BF)
    rank = jnp.dot(before, named.astype(BF), preferred_element_type=F32)
    seat = named * (rank + 1.0)
    at = jnp.dot(seat.astype(BF), _spread(), preferred_element_type=F32)
    tok = lax.broadcasted_iota(jnp.int32, (TOKS, ROWS), 0)
    slot = lax.broadcasted_iota(jnp.int32, (TOKS, ROWS), 1)
    return (at == (slot % 2 + 1).astype(F32)) & (tok // TOK == (slot % 16) // 2)


def _select_kernel(z_ref, m_ref, t_ref, *rest):
    o_ref = rest[-1]
    slots = _slots(_matches(m_ref[...].reshape(TOKS, META).astype(F32), z_ref[0])).astype(BF)
    t = t_ref[...].reshape(TOKS, t_ref.shape[2])
    out = lax.dot_general(slots, t, (((0,), (0,)), ((), ())), preferred_element_type=F32)
    o_ref[...] = out.astype(BF).reshape(o_ref.shape)


def _select(z1, table, after):
    width = (WIDE + META) // 3
    return pl.pallas_call(
        _select_kernel,
        grid_spec=pltpu.PrefetchScalarGridSpec(
            num_scalar_prefetch=1,
            grid=(3,),
            in_specs=[
                pl.BlockSpec((8, TOK, META), lambda g, z: (0, 0, WIDE // META)),
                pl.BlockSpec((8, TOK, width), lambda g, z: (0, 0, g)),
            ]
            + [pl.BlockSpec(memory_space=pl.ANY) for _ in after],
            out_specs=pl.BlockSpec((DEST, 16, width), lambda g, z: (0, 0, g)),
        ),
        out_shape=jax.ShapeDtypeStruct((DEST, 16, WIDE + META), BF),
        compiler_params=_params(24),
        name="select",
    )(z1, table, table, *after)


HELD = (
    (0, 0, 256, 0, 0, 0),
    (0, 256, 512, 0, 1, 0),
    (1, 0, 256, 3, 0, 0),
    (1, 256, 512, 3, 1, 0),
    (2, 0, 256, 1, 0, 0),
    (2, 256, 512, 1, 1, 0),
    (3, 0, 256, 2, 0, 0),
    (3, 256, 128, 2, 1, 0),
    (4, 0, 384, 2, 1, 128),
)


def _up_kernel(at, x_ref, *refs):
    w = refs[:5]
    w_own, a_in, a_out, o_ref, high, low, hidden = refs[5:]
    g = pl.program_id(0)

    @pl.when(g == 0)
    def _():
        kept = jnp.zeros((ROWS, 64), F32)
        for i in range(8):
            part = x_ref[:, i * 512 : i * 512 + 512]
            kept += lax.dot_general(part, a_in[i, 0], (((1,), (1,)), ((), ())), preferred_element_type=F32)
        kept *= x_ref[:, WIDE : WIDE + 64].astype(F32)
        high[...] = kept.astype(BF)
        low[...] = (kept - high[...].astype(F32)).astype(BF)

    v = jnp.dot(high[...], a_out[0], preferred_element_type=F32)
    v += jnp.dot(low[...], a_out[0], preferred_element_type=F32)
    for held, row, size, away, side, start in HELD:
        core = at[0] if side == 0 else 1 - at[0]
        first = pl.multiple_of(lax.rem(at[1] + away, 4) * PIECE + core * 512 + start, 128)
        v += jnp.dot(x_ref[:, pl.ds(first, size)], w[held][row : row + size], preferred_element_type=F32)
    for i in range(4):
        first = pl.multiple_of(i * PIECE + at[0] * 512 + 256, 128)
        v += jnp.dot(x_ref[:, pl.ds(first, 256)], w_own[i], preferred_element_type=F32)
    hidden[g] = (v / (1.0 + jnp.exp(-v))).astype(BF).astype(F32)

    @pl.when(g == 3)
    def _():
        peak = jnp.max(jnp.abs(hidden[0]), axis=1, keepdims=True)
        for i in range(1, 4):
            peak = jnp.maximum(peak, jnp.max(jnp.abs(hidden[i]), axis=1, keepdims=True))
        power = jnp.floor(jnp.log2(jnp.maximum(peak, 1e-30)))
        scale = jnp.exp2(-power)
        for i in range(4):
            o_ref[:, i * 256 : i * 256 + 256] = (hidden[i] * scale).astype(BF)
        o_ref[:, PIECE:] = jnp.broadcast_to(power, (ROWS, META)).astype(BF)


def _up(at, rows, w_own, w, a_in, a_out):
    return pl.pallas_call(
        _up_kernel,
        grid_spec=pltpu.PrefetchScalarGridSpec(
            num_scalar_prefetch=1,
            grid=(4,),
            in_specs=[pl.BlockSpec((ROWS, WIDE + META), lambda g, at: (0, 0))]
            + [pl.BlockSpec((p.shape[0], 256), lambda g, at: (0, g)) for p in w]
            + [
                pl.BlockSpec((4, 256, 256), lambda g, at: (0, 0, g)),
                pl.BlockSpec((8, 1, 64, 512), lambda g, at: (0, at[0], 0, 0)),
                pl.BlockSpec((1, 64, 256), lambda g, at: (at[0], 0, g)),
            ],
            out_specs=pl.BlockSpec((ROWS, PIECE + META), lambda g, at: (0, 0)),
            scratch_shapes=[
                pltpu.VMEM((ROWS, 64), BF),
                pltpu.VMEM((ROWS, 64), BF),
                pltpu.VMEM((4, ROWS, 256), F32),
            ],
        ),
        out_shape=jax.ShapeDtypeStruct((ROWS, PIECE + META), BF),
        compiler_params=_params(32),
        name="up",
    )(at, rows, *w, w_own, a_in, a_out)


def _down_kernel(c_ref, h_ref, m_ref, w_own, w_other, o_ref):
    scale = jnp.exp2(m_ref[0, :, :1].astype(F32))
    for side, w in ((c_ref[0], w_own[0]), (1 - c_ref[0], w_other[...])):
        cols = pl.ds(pl.multiple_of(side * 512, 512), 512)
        out = jnp.dot(h_ref[0], w, preferred_element_type=F32) * scale
        o_ref[:, :, :, cols] = out.astype(BF).reshape(1, DEST, 16, 512)


def _down(c, hidden, w, w_other):
    return pl.pallas_call(
        _down_kernel,
        grid_spec=pltpu.PrefetchScalarGridSpec(
            num_scalar_prefetch=1,
            grid=(4,),
            in_specs=[
                pl.BlockSpec((1, ROWS, PIECE), lambda g, c: (g, 0, 0)),
                pl.BlockSpec((1, ROWS, META), lambda g, c: (g, 0, PIECE // META)),
                pl.BlockSpec((1, PIECE, 512), lambda g, c: (c[0], 0, 0)),
                pl.BlockSpec((PIECE, 512), lambda g, c: (0, 0)),
            ],
            out_specs=pl.BlockSpec((1, DEST, 16, PIECE), lambda g, c: (g, 0, 0, 0)),
        ),
        out_shape=jax.ShapeDtypeStruct((4, DEST, 16, PIECE), BF),
        compiler_params=_params(24),
        name="down",
    )(c, hidden, hidden, w, w_other)


def _combine_kernel(z_ref, m_ref, y_ref, o_ref, weight):
    @pl.when(pl.program_id(0) == 0)
    def _():
        meta = m_ref[...].reshape(TOKS, META).astype(F32)
        matches = _matches(meta, z_ref[0])
        gate = sum(jnp.where(m, meta[:, GATE_AT + k : GATE_AT + k + 1], 0.0) for k, m in enumerate(matches))
        gates = jnp.dot(gate.astype(BF), _spread(), preferred_element_type=F32)
        weight[...] = jnp.where(_slots(matches), gates, 0.0).astype(BF)

    out = jnp.dot(weight[...], y_ref[...].reshape(ROWS, PIECE), preferred_element_type=F32)
    o_ref[...] = out.astype(BF)


def _combine(z1, table, back):
    return pl.pallas_call(
        _combine_kernel,
        grid_spec=pltpu.PrefetchScalarGridSpec(
            num_scalar_prefetch=1,
            grid=(4,),
            in_specs=[
                pl.BlockSpec((8, TOK, META), lambda g, z: (0, 0, WIDE // META)),
                pl.BlockSpec((1, DEST, 16, PIECE), lambda g, z: (g, 0, 0, 0)),
            ],
            out_specs=pl.BlockSpec((TOKS, PIECE), lambda g, z: (0, g)),
            scratch_shapes=[pltpu.VMEM((TOKS, ROWS), BF)],
        ),
        out_shape=jax.ShapeDtypeStruct((TOKS, WIDE), BF),
        compiler_params=_params(24),
        name="combine",
    )(z1, table, back)


def _shift_x(v, by):
    return lax.ppermute(v, "x", [(i, (i + by) % 4) for i in range(4)])


def _gather_x(w):
    left, right = _shift_x(w, 1), _shift_x(w, -1)
    return [w, left, right, _shift_x(left[:384], 1), _shift_x(right[384:], -1)]


def _swap(v):
    return lax.ppermute(v, "core", [(0, 1), (1, 0)])


def per_device(tokens, route_ids, gate_weights, tenant_ids, up_weight, down_weight, adapter_in, adapter_out):
    z1 = lax.axis_index("z1").astype(jnp.int32).reshape(1)
    core = lax.axis_index("core").astype(jnp.int32)
    c = core.reshape(1)
    at = jnp.stack([core, lax.axis_index("x").astype(jnp.int32)])
    one = lambda w, i: lax.dynamic_index_in_dim(w, i, 0, keepdims=False)

    up_own, up_other = one(up_weight, core), _swap(one(up_weight, 1 - core))
    w_own = lax.all_gather(up_own[256:], "x", axis=0)
    w_up = _gather_x(jnp.concatenate([up_own[:256], up_other], axis=0))
    a_in = lax.all_gather(adapter_in.transpose(0, 2, 1), ("x", "core"), axis=0)
    down_other = _swap(one(down_weight, 1 - core))

    owner = jnp.arange(TEN * RANK, dtype=jnp.int32) // RANK
    mask = (owner[None, :] == tenant_ids[:, None]).astype(F16)
    meta = jnp.concatenate(
        [mask, route_ids.astype(F16), gate_weights.astype(F16), jnp.zeros((TOK, META - 80), F16)], axis=1
    )
    mine = jnp.concatenate([(tokens.astype(F32) * LIFT).astype(F16), meta], axis=1)
    table = lax.all_gather(mine, "z1", axis=0).astype(F32)
    lift = jnp.where(jnp.arange(WIDE + META) < WIDE, 1.0 / LIFT, 1.0)
    table = (table * lift).astype(BF)
    sending = _select(z1, table, w_up[1:3] + [w_own])
    arrived = lax.all_to_all(sending, ("y", "core", "z0"), 0, 0, tiled=True).reshape(ROWS, WIDE + META)

    hidden = _up(at, arrived, w_own, w_up, a_in, adapter_out)
    hidden = lax.all_gather(hidden.astype(F16), "x", axis=0).astype(BF)
    out = _down(c, hidden, down_weight, down_other)
    back = lax.all_to_all(out.reshape(64, 16, PIECE), ("x", "y", "core", "z0"), 0, 0, tiled=True)
    partial = _combine(z1, table, back.reshape(4, DEST, 16, PIECE))
    return lax.psum_scatter(partial, "z1", scatter_dimension=0, tiled=True)


def solution(mesh):
    fine = Mesh(mesh.devices.reshape(4, 2, 8, 2, 4), ("x", "core", "z1", "z0", "y"))
    dp, ex = ("x", "core"), ("z1", "z0", "y")
    every = dp + ex
    placed = (
        P(every, None),
        P(every, None),
        P(every, None),
        P(every),
        P(ex, dp, None),
        P(ex, None, dp),
        P(ex, dp, None),
        P(ex, None, None),
    )
    return jax.shard_map(per_device, mesh=fine, in_specs=placed, out_specs=P(every, None), check_vma=False)
```

```python
import jax
import jax.numpy as jnp
from jax import lax
from jax.experimental import pallas as pl
from jax.experimental.pallas import tpu as pltpu
from jax.sharding import Mesh, PartitionSpec as P

BF = jnp.bfloat16
F16 = jnp.float16
F32 = jnp.float32
TOK = 16
TOP = 8
DEST = 16
TEN = 4
RANK = 16
PIECE = 1024
WIDE = 4096
META = 128
ROUTE_AT = 64
GATE_AT = 72
ROWS = 256
TOKS = 128
LIFT = 4096.0
def _params(mib):
    return pltpu.CompilerParams(vmem_limit_bytes=mib << 20)


def _matches(meta, z1):
    lane = lax.broadcasted_iota(jnp.int32, (TOKS, META), 1)
    expert = (z1 * 2 + lane % 2) * 8 + (lane // 4) * 2 + (lane // 2) % 2
    expert = jnp.where(lane < DEST, expert, -1).astype(F32)
    return [meta[:, ROUTE_AT + k : ROUTE_AT + k + 1] == expert for k in range(TOP)]


def _spread():
    e = lax.broadcasted_iota(jnp.int32, (META, ROWS), 0)
    j = lax.broadcasted_iota(jnp.int32, (META, ROWS), 1)
    return (e == j // 16).astype(BF)


def _slots(matches):
    named = sum(m.astype(F32) for m in matches)
    row = lax.broadcasted_iota(jnp.int32, (TOKS, TOKS), 0)
    col = lax.broadcasted_iota(jnp.int32, (TOKS, TOKS), 1)
    before = ((row // TOK == col // TOK) & (col < row)).astype(BF)
    rank = jnp.dot(before, named.astype(BF), preferred_element_type=F32)
    seat = named * (rank + 1.0)
    at = jnp.dot(seat.astype(BF), _spread(), preferred_element_type=F32)
    tok = lax.broadcasted_iota(jnp.int32, (TOKS, ROWS), 0)
    slot = lax.broadcasted_iota(jnp.int32, (TOKS, ROWS), 1)
    return (at == (slot % 2 + 1).astype(F32)) & (tok // TOK == (slot % 16) // 2)


def _select_kernel(z_ref, m_ref, t_ref, left, right, after, o_ref, low, high, sem):
    g = pl.program_id(0)
    copies = (
        pltpu.make_async_copy(left.at[pl.ds(0, 512)], low, sem.at[0]),
        pltpu.make_async_copy(right.at[pl.ds(512, 512)], high, sem.at[1]),
    )

    @pl.when(g == 0)
    def _():
        for copy in copies:
            copy.start()

    slots = _slots(_matches(m_ref[...].reshape(TOKS, META).astype(F32), z_ref[0])).astype(BF)
    t = t_ref[...].reshape(TOKS, t_ref.shape[2])
    out = lax.dot_general(slots, t, (((0,), (0,)), ((), ())), preferred_element_type=F32)
    o_ref[...] = out.astype(BF).reshape(o_ref.shape)

    @pl.when(g == 2)
    def _():
        for copy in copies:
            copy.wait()


def _select(z1, table, left, right, after):
    width = (WIDE + META) // 3
    anywhere = pl.BlockSpec(memory_space=pl.ANY)
    half = jax.ShapeDtypeStruct((512, PIECE), BF)
    return pl.pallas_call(
        _select_kernel,
        grid_spec=pltpu.PrefetchScalarGridSpec(
            num_scalar_prefetch=1,
            grid=(3,),
            in_specs=[
                pl.BlockSpec((8, TOK, META), lambda g, z: (0, 0, WIDE // META)),
                pl.BlockSpec((8, TOK, width), lambda g, z: (0, 0, g)),
                anywhere,
                anywhere,
                anywhere,
            ],
            out_specs=[pl.BlockSpec((DEST, 16, width), lambda g, z: (0, 0, g)), anywhere, anywhere],
            scratch_shapes=[pltpu.SemaphoreType.DMA((2,))],
        ),
        out_shape=[jax.ShapeDtypeStruct((DEST, 16, WIDE + META), BF), half, half],
        compiler_params=_params(56),
        name="select",
    )(z1, table, table, left, right, after)


HELD = ((0, 0, 1024), (3, 0, 1024), (1, 0, 1024), (2, 0, 512), (2, 512, 512))


def _up_kernel(at, x_ref, *refs):
    w = refs[: len(HELD)]
    a_in, a_out, o_ref, high, low, hidden = refs[len(HELD) :]
    g = pl.program_id(0)

    @pl.when(g == 0)
    def _():
        kept = jnp.zeros((ROWS, 64), F32)
        for i in range(8):
            part = x_ref[:, i * 512 : i * 512 + 512]
            kept += lax.dot_general(part, a_in[i, 0], (((1,), (1,)), ((), ())), preferred_element_type=F32)
        kept *= x_ref[:, WIDE : WIDE + 64].astype(F32)
        high[...] = kept.astype(BF)
        low[...] = (kept - high[...].astype(F32)).astype(BF)

    v = jnp.dot(high[...], a_out[0], preferred_element_type=F32)
    v += jnp.dot(low[...], a_out[0], preferred_element_type=F32)
    for ref, (away, start, size) in zip(w, HELD):
        first = pl.multiple_of(lax.rem(at[1] + away, 4) * PIECE + start, 256)
        v += jnp.dot(x_ref[:, pl.ds(first, size)], ref[...], preferred_element_type=F32)
    hidden[g] = (v / (1.0 + jnp.exp(-v))).astype(BF).astype(F32)

    @pl.when(g == 3)
    def _():
        peak = jnp.max(jnp.abs(hidden[0]), axis=1, keepdims=True)
        for i in range(1, 4):
            peak = jnp.maximum(peak, jnp.max(jnp.abs(hidden[i]), axis=1, keepdims=True))
        power = jnp.floor(jnp.log2(jnp.maximum(peak, 1e-30)))
        scale = jnp.exp2(-power)
        for i in range(4):
            o_ref[:, i * 256 : i * 256 + 256] = (hidden[i] * scale).astype(BF)
        o_ref[:, PIECE:] = jnp.broadcast_to(power, (ROWS, META)).astype(BF)


def _up(at, rows, w, a_in, a_out):
    return pl.pallas_call(
        _up_kernel,
        grid_spec=pltpu.PrefetchScalarGridSpec(
            num_scalar_prefetch=1,
            grid=(4,),
            in_specs=[pl.BlockSpec((ROWS, WIDE + META), lambda g, at: (0, 0))]
            + [pl.BlockSpec((p.shape[0], 256), lambda g, at: (0, g)) for p in w]
            + [
                pl.BlockSpec((8, 1, 64, 512), lambda g, at: (0, at[0], 0, 0)),
                pl.BlockSpec((1, 64, 256), lambda g, at: (at[0], 0, g)),
            ],
            out_specs=pl.BlockSpec((ROWS, PIECE + META), lambda g, at: (0, 0)),
            scratch_shapes=[
                pltpu.VMEM((ROWS, 64), BF),
                pltpu.VMEM((ROWS, 64), BF),
                pltpu.VMEM((4, ROWS, 256), F32),
            ],
        ),
        out_shape=jax.ShapeDtypeStruct((ROWS, PIECE + META), BF),
        compiler_params=_params(56),
        name="up",
    )(at, rows, *w, a_in, a_out)


def _down_kernel(c_ref, h_ref, m_ref, w_own, w_other, o_ref):
    scale = jnp.exp2(m_ref[0, :, :1].astype(F32))
    for side, w in ((c_ref[0], w_own[0]), (1 - c_ref[0], w_other[...])):
        cols = pl.ds(pl.multiple_of(side * 512, 512), 512)
        out = jnp.dot(h_ref[0], w, preferred_element_type=F32) * scale
        o_ref[:, :, :, cols] = out.astype(BF).reshape(1, DEST, 16, 512)


def _down(c, hidden, w, w_other):
    return pl.pallas_call(
        _down_kernel,
        grid_spec=pltpu.PrefetchScalarGridSpec(
            num_scalar_prefetch=1,
            grid=(4,),
            in_specs=[
                pl.BlockSpec((1, ROWS, PIECE), lambda g, c: (g, 0, 0)),
                pl.BlockSpec((1, ROWS, META), lambda g, c: (g, 0, PIECE // META)),
                pl.BlockSpec((1, PIECE, 512), lambda g, c: (c[0], 0, 0)),
                pl.BlockSpec((PIECE, 512), lambda g, c: (0, 0)),
            ],
            out_specs=pl.BlockSpec((1, DEST, 16, PIECE), lambda g, c: (g, 0, 0, 0)),
        ),
        out_shape=jax.ShapeDtypeStruct((4, DEST, 16, PIECE), BF),
        compiler_params=_params(56),
        name="down",
    )(c, hidden, hidden, w, w_other)


def _combine_kernel(z_ref, m_ref, y_ref, o_ref, weight):
    @pl.when(pl.program_id(0) == 0)
    def _():
        meta = m_ref[...].reshape(TOKS, META).astype(F32)
        matches = _matches(meta, z_ref[0])
        gate = sum(jnp.where(m, meta[:, GATE_AT + k : GATE_AT + k + 1], 0.0) for k, m in enumerate(matches))
        gates = jnp.dot(gate.astype(BF), _spread(), preferred_element_type=F32)
        weight[...] = jnp.where(_slots(matches), gates, 0.0).astype(BF)

    out = jnp.dot(weight[...], y_ref[...].reshape(ROWS, PIECE), preferred_element_type=F32)
    o_ref[...] = out.astype(BF)


def _combine(z1, table, back):
    return pl.pallas_call(
        _combine_kernel,
        grid_spec=pltpu.PrefetchScalarGridSpec(
            num_scalar_prefetch=1,
            grid=(4,),
            in_specs=[
                pl.BlockSpec((8, TOK, META), lambda g, z: (0, 0, WIDE // META)),
                pl.BlockSpec((1, DEST, 16, PIECE), lambda g, z: (g, 0, 0, 0)),
            ],
            out_specs=pl.BlockSpec((TOKS, PIECE), lambda g, z: (0, g)),
            scratch_shapes=[pltpu.VMEM((TOKS, ROWS), BF)],
        ),
        out_shape=jax.ShapeDtypeStruct((TOKS, WIDE), BF),
        compiler_params=_params(56),
        name="combine",
    )(z1, table, back)


def _shift_x(v, by):
    return lax.ppermute(v, "x", [(i, (i + by) % 4) for i in range(4)])


def _swap(v):
    return lax.ppermute(v, "core", [(0, 1), (1, 0)])


def per_device(tokens, route_ids, gate_weights, tenant_ids, up_weight, down_weight, adapter_in, adapter_out):
    z1 = lax.axis_index("z1").astype(jnp.int32).reshape(1)
    core = lax.axis_index("core").astype(jnp.int32)
    c = core.reshape(1)
    at = jnp.stack([core, lax.axis_index("x").astype(jnp.int32)])
    one = lambda w, i: lax.dynamic_index_in_dim(w, i, 0, keepdims=False)

    up_own, up_other = one(up_weight, core), _swap(one(up_weight, 1 - core))
    first, second = jnp.where(core == 0, up_own, up_other), jnp.where(core == 0, up_other, up_own)
    block = jnp.concatenate([first, second], axis=0)
    left, right = _shift_x(block, 1), _shift_x(block, -1)
    a_in = lax.all_gather(adapter_in.transpose(0, 2, 1), ("x", "core"), axis=0)
    down_other = _swap(one(down_weight, 1 - core))

    owner = jnp.arange(TEN * RANK, dtype=jnp.int32) // RANK
    mask = (owner[None, :] == tenant_ids[:, None]).astype(F16)
    meta = jnp.concatenate(
        [mask, route_ids.astype(F16), gate_weights.astype(F16), jnp.zeros((TOK, META - 80), F16)], axis=1
    )
    mine = jnp.concatenate([(tokens.astype(F32) * LIFT).astype(F16), meta], axis=1)
    table = lax.all_gather(mine, "z1", axis=0).astype(F32)
    lift = jnp.where(jnp.arange(WIDE + META) < WIDE, 1.0 / LIFT, 1.0)
    table = (table * lift).astype(BF)
    sending, low, high = _select(z1, table, left, right, a_in)
    w_up = [block, left, right, _shift_x(low, 1), _shift_x(high, -1)]
    arrived = lax.all_to_all(sending, ("y", "core", "z0"), 0, 0, tiled=True).reshape(ROWS, WIDE + META)

    hidden = _up(at, arrived, w_up, a_in, adapter_out)
    hidden = lax.all_gather(hidden.astype(F16), "x", axis=0).astype(BF)
    out = _down(c, hidden, down_weight, down_other)
    back = lax.all_to_all(out.reshape(64, 16, PIECE), ("x", "y", "core", "z0"), 0, 0, tiled=True)
    partial = _combine(z1, table, back.reshape(4, DEST, 16, PIECE))
    return lax.psum_scatter(partial, "z1", scatter_dimension=0, tiled=True)


def solution(mesh):
    fine = Mesh(mesh.devices.reshape(4, 2, 8, 2, 4), ("x", "core", "z1", "z0", "y"))
    dp, ex = ("x", "core"), ("z1", "z0", "y")
    every = dp + ex
    placed = (
        P(every, None),
        P(every, None),
        P(every, None),
        P(every),
        P(ex, dp, None),
        P(ex, None, dp),
        P(ex, dp, None),
        P(ex, None, None),
    )
    return jax.shard_map(per_device, mesh=fine, in_specs=placed, out_specs=P(every, None), check_vma=False)
```

```python
import jax
import jax.numpy as jnp
from jax import lax
from jax.experimental import pallas as pl
from jax.experimental.pallas import tpu as pltpu
from jax.sharding import Mesh, PartitionSpec as P

BF = jnp.bfloat16
F16 = jnp.float16
F32 = jnp.float32
TOK = 16
TOP = 8
DEST = 16
TEN = 4
RANK = 16
PIECE = 1024
WIDE = 4096
META = 128
ROUTE_AT = 64
GATE_AT = 72
ROWS = 256
TOKS = 128
LIFT = 4096.0
def _params(mib):
    return pltpu.CompilerParams(vmem_limit_bytes=mib << 20)


def _matches(meta, z1):
    lane = lax.broadcasted_iota(jnp.int32, (TOKS, META), 1)
    expert = (z1 * 2 + lane % 2) * 8 + (lane // 4) * 2 + (lane // 2) % 2
    expert = jnp.where(lane < DEST, expert, -1).astype(F32)
    return [meta[:, ROUTE_AT + k : ROUTE_AT + k + 1] == expert for k in range(TOP)]


def _spread():
    e = lax.broadcasted_iota(jnp.int32, (META, ROWS), 0)
    j = lax.broadcasted_iota(jnp.int32, (META, ROWS), 1)
    return (e == j // 16).astype(BF)


def _slots(matches):
    named = sum(m.astype(F32) for m in matches)
    row = lax.broadcasted_iota(jnp.int32, (TOKS, TOKS), 0)
    col = lax.broadcasted_iota(jnp.int32, (TOKS, TOKS), 1)
    before = ((row // TOK == col // TOK) & (col < row)).astype(BF)
    rank = jnp.dot(before, named.astype(BF), preferred_element_type=F32)
    seat = named * (rank + 1.0)
    at = jnp.dot(seat.astype(BF), _spread(), preferred_element_type=F32)
    tok = lax.broadcasted_iota(jnp.int32, (TOKS, ROWS), 0)
    slot = lax.broadcasted_iota(jnp.int32, (TOKS, ROWS), 1)
    return (at == (slot % 2 + 1).astype(F32)) & (tok // TOK == (slot % 16) // 2)


def _select_kernel(z_ref, m_ref, t_ref, left, right, after, o_ref, low, high):
    slots = _slots(_matches(m_ref[...].reshape(TOKS, META).astype(F32), z_ref[0])).astype(BF)
    t = t_ref[...].reshape(TOKS, t_ref.shape[2])
    out = lax.dot_general(slots, t, (((0,), (0,)), ((), ())), preferred_element_type=F32)
    o_ref[...] = out.astype(BF).reshape(o_ref.shape)

    @pl.when(pl.program_id(0) == 0)
    def _():
        low[...] = left[...]
        high[...] = right[...]


def _select(z1, table, left, right, after):
    width = (WIDE + META) // 3
    upper = pl.BlockSpec((512, PIECE), lambda g, z: (0, 0))
    half = jax.ShapeDtypeStruct((512, PIECE), BF)
    return pl.pallas_call(
        _select_kernel,
        grid_spec=pltpu.PrefetchScalarGridSpec(
            num_scalar_prefetch=1,
            grid=(3,),
            in_specs=[
                pl.BlockSpec((8, TOK, META), lambda g, z: (0, 0, WIDE // META)),
                pl.BlockSpec((8, TOK, width), lambda g, z: (0, 0, g)),
                upper,
                pl.BlockSpec((512, PIECE), lambda g, z: (1, 0)),
                pl.BlockSpec(memory_space=pl.ANY),
            ],
            out_specs=[pl.BlockSpec((DEST, 16, width), lambda g, z: (0, 0, g)), upper, upper],
        ),
        out_shape=[jax.ShapeDtypeStruct((DEST, 16, WIDE + META), BF), half, half],
        compiler_params=_params(24),
        name="select",
    )(z1, table, table, left, right, after)


HELD = ((0, 0, 1024), (3, 0, 1024), (1, 0, 1024), (2, 0, 512), (2, 512, 512))


def _up_kernel(at, x_ref, *refs):
    w = refs[: len(HELD)]
    a_in, a_out, o_ref, high, low, hidden = refs[len(HELD) :]
    g = pl.program_id(0)

    @pl.when(g == 0)
    def _():
        kept = jnp.zeros((ROWS, 64), F32)
        for i in range(8):
            part = x_ref[:, i * 512 : i * 512 + 512]
            kept += lax.dot_general(part, a_in[i, 0], (((1,), (1,)), ((), ())), preferred_element_type=F32)
        kept *= x_ref[:, WIDE : WIDE + 64].astype(F32)
        high[...] = kept.astype(BF)
        low[...] = (kept - high[...].astype(F32)).astype(BF)

    v = jnp.dot(high[...], a_out[0], preferred_element_type=F32)
    v += jnp.dot(low[...], a_out[0], preferred_element_type=F32)
    for ref, (away, start, size) in zip(w, HELD):
        first = pl.multiple_of(lax.rem(at[1] + away, 4) * PIECE + start, 256)
        v += jnp.dot(x_ref[:, pl.ds(first, size)], ref[...], preferred_element_type=F32)
    hidden[g] = (v / (1.0 + jnp.exp(-v))).astype(BF).astype(F32)

    @pl.when(g == 3)
    def _():
        peak = jnp.max(jnp.abs(hidden[0]), axis=1, keepdims=True)
        for i in range(1, 4):
            peak = jnp.maximum(peak, jnp.max(jnp.abs(hidden[i]), axis=1, keepdims=True))
        power = jnp.floor(jnp.log2(jnp.maximum(peak, 1e-30)))
        scale = jnp.exp2(-power)
        for i in range(4):
            o_ref[:, i * 256 : i * 256 + 256] = (hidden[i] * scale).astype(BF)
        o_ref[:, PIECE:] = jnp.broadcast_to(power, (ROWS, META)).astype(BF)


def _up(at, rows, w, a_in, a_out):
    return pl.pallas_call(
        _up_kernel,
        grid_spec=pltpu.PrefetchScalarGridSpec(
            num_scalar_prefetch=1,
            grid=(4,),
            in_specs=[pl.BlockSpec((ROWS, WIDE + META), lambda g, at: (0, 0))]
            + [pl.BlockSpec((p.shape[0], 256), lambda g, at: (0, g)) for p in w]
            + [
                pl.BlockSpec((8, 1, 64, 512), lambda g, at: (0, at[0], 0, 0)),
                pl.BlockSpec((1, 64, 256), lambda g, at: (at[0], 0, g)),
            ],
            out_specs=pl.BlockSpec((ROWS, PIECE + META), lambda g, at: (0, 0)),
            scratch_shapes=[
                pltpu.VMEM((ROWS, 64), BF),
                pltpu.VMEM((ROWS, 64), BF),
                pltpu.VMEM((4, ROWS, 256), F32),
            ],
        ),
        out_shape=jax.ShapeDtypeStruct((ROWS, PIECE + META), BF),
        compiler_params=_params(28),
        name="up",
    )(at, rows, *w, a_in, a_out)


def _down_kernel(c_ref, h_ref, m_ref, w_own, w_other, o_ref):
    scale = jnp.exp2(m_ref[0, :, :1].astype(F32))
    for side, w in ((c_ref[0], w_own[0]), (1 - c_ref[0], w_other[...])):
        cols = pl.ds(pl.multiple_of(side * 512, 512), 512)
        out = jnp.dot(h_ref[0], w, preferred_element_type=F32) * scale
        o_ref[:, :, :, cols] = out.astype(BF).reshape(1, DEST, 16, 512)


def _down(c, hidden, w, w_other):
    return pl.pallas_call(
        _down_kernel,
        grid_spec=pltpu.PrefetchScalarGridSpec(
            num_scalar_prefetch=1,
            grid=(4,),
            in_specs=[
                pl.BlockSpec((1, ROWS, PIECE), lambda g, c: (g, 0, 0)),
                pl.BlockSpec((1, ROWS, META), lambda g, c: (g, 0, PIECE // META)),
                pl.BlockSpec((1, PIECE, 512), lambda g, c: (c[0], 0, 0)),
                pl.BlockSpec((PIECE, 512), lambda g, c: (0, 0)),
            ],
            out_specs=pl.BlockSpec((1, DEST, 16, PIECE), lambda g, c: (g, 0, 0, 0)),
        ),
        out_shape=jax.ShapeDtypeStruct((4, DEST, 16, PIECE), BF),
        compiler_params=_params(28),
        name="down",
    )(c, hidden, hidden, w, w_other)


def _combine_kernel(z_ref, m_ref, y_ref, o_ref, weight):
    @pl.when(pl.program_id(0) == 0)
    def _():
        meta = m_ref[...].reshape(TOKS, META).astype(F32)
        matches = _matches(meta, z_ref[0])
        gate = sum(jnp.where(m, meta[:, GATE_AT + k : GATE_AT + k + 1], 0.0) for k, m in enumerate(matches))
        gates = jnp.dot(gate.astype(BF), _spread(), preferred_element_type=F32)
        weight[...] = jnp.where(_slots(matches), gates, 0.0).astype(BF)

    out = jnp.dot(weight[...], y_ref[...].reshape(ROWS, PIECE), preferred_element_type=F32)
    o_ref[...] = out.astype(BF)


def _combine(z1, table, back):
    return pl.pallas_call(
        _combine_kernel,
        grid_spec=pltpu.PrefetchScalarGridSpec(
            num_scalar_prefetch=1,
            grid=(4,),
            in_specs=[
                pl.BlockSpec((8, TOK, META), lambda g, z: (0, 0, WIDE // META)),
                pl.BlockSpec((1, DEST, 16, PIECE), lambda g, z: (g, 0, 0, 0)),
            ],
            out_specs=pl.BlockSpec((TOKS, PIECE), lambda g, z: (0, g)),
            scratch_shapes=[pltpu.VMEM((TOKS, ROWS), BF)],
        ),
        out_shape=jax.ShapeDtypeStruct((TOKS, WIDE), BF),
        compiler_params=_params(28),
        name="combine",
    )(z1, table, back)


def _shift_x(v, by):
    return lax.ppermute(v, "x", [(i, (i + by) % 4) for i in range(4)])


def _swap(v):
    return lax.ppermute(v, "core", [(0, 1), (1, 0)])


def per_device(tokens, route_ids, gate_weights, tenant_ids, up_weight, down_weight, adapter_in, adapter_out):
    z1 = lax.axis_index("z1").astype(jnp.int32).reshape(1)
    core = lax.axis_index("core").astype(jnp.int32)
    c = core.reshape(1)
    at = jnp.stack([core, lax.axis_index("x").astype(jnp.int32)])
    one = lambda w, i: lax.dynamic_index_in_dim(w, i, 0, keepdims=False)

    up_own, up_other = one(up_weight, core), _swap(one(up_weight, 1 - core))
    first, second = jnp.where(core == 0, up_own, up_other), jnp.where(core == 0, up_other, up_own)
    block = jnp.concatenate([first, second], axis=0)
    left, right = _shift_x(block, 1), _shift_x(block, -1)
    a_in = lax.all_gather(adapter_in.transpose(0, 2, 1), ("x", "core"), axis=0)
    down_other = _swap(one(down_weight, 1 - core))

    owner = jnp.arange(TEN * RANK, dtype=jnp.int32) // RANK
    mask = (owner[None, :] == tenant_ids[:, None]).astype(F16)
    meta = jnp.concatenate(
        [mask, route_ids.astype(F16), gate_weights.astype(F16), jnp.zeros((TOK, META - 80), F16)], axis=1
    )
    mine = jnp.concatenate([(tokens.astype(F32) * LIFT).astype(F16), meta], axis=1)
    table = lax.all_gather(mine, "z1", axis=0).astype(F32)
    lift = jnp.where(jnp.arange(WIDE + META) < WIDE, 1.0 / LIFT, 1.0)
    table = (table * lift).astype(BF)
    sending, low, high = _select(z1, table, left, right, a_in)
    w_up = [block, left, right, _shift_x(low, 1), _shift_x(high, -1)]
    arrived = lax.all_to_all(sending, ("y", "core", "z0"), 0, 0, tiled=True).reshape(ROWS, WIDE + META)

    hidden = _up(at, arrived, w_up, a_in, adapter_out)
    hidden = lax.all_gather(hidden.astype(F16), "x", axis=0).astype(BF)
    out = _down(c, hidden, down_weight, down_other)
    back = lax.all_to_all(out.reshape(64, 16, PIECE), ("x", "y", "core", "z0"), 0, 0, tiled=True)
    partial = _combine(z1, table, back.reshape(4, DEST, 16, PIECE))
    return lax.psum_scatter(partial, "z1", scatter_dimension=0, tiled=True)


def solution(mesh):
    fine = Mesh(mesh.devices.reshape(4, 2, 8, 2, 4), ("x", "core", "z1", "z0", "y"))
    dp, ex = ("x", "core"), ("z1", "z0", "y")
    every = dp + ex
    placed = (
        P(every, None),
        P(every, None),
        P(every, None),
        P(every),
        P(ex, dp, None),
        P(ex, None, dp),
        P(ex, dp, None),
        P(ex, None, None),
    )
    return jax.shard_map(per_device, mesh=fine, in_specs=placed, out_specs=P(every, None), check_vma=False)
```
